32 devices in a mesh: role: 2 (over x), dp: 4 (over y, core), vocab: 4 (over z).
Axes of the slice: x: 2, y: 2, z: 4, core: 2. Of those that a mesh axis runs over, the one named last changes fastest.
Arguments:
- hidden: bfloat16 [4096, 1792], P(('role', 'dp'))
- out_weight: bfloat16 [1792, 9728], P(None, 'vocab')
- teacher_logits: bfloat16 [4096, 9728], P(('role', 'dp'), 'vocab')
- token_ids: int32 [4096], P(('role', 'dp')), may hold values from 0 to 9727
- loss_mask: int32 [4096], P(('role', 'dp')), may hold values from 0 to 1
Outputs:
- token_kl: float32 [4096], P(('role', 'dp'))
- chosen_logprob: float32 [4096], P(('role', 'dp'))
- grad_hidden: bfloat16 [4096, 1792], P(('role', 'dp', 'vocab'))
- grad_weight: bfloat16 [1792, 9728], P(('role', 'dp'), 'vocab')
The draws below stay inside these ranges and needn't reach their ends.
All inputs are finite; a program needn't handle non-finite values.
Results may differ from the reference program's by a relative error of at most 0.02.
Values may be sent and summed in bfloat16 or wider, within the bound.
No kernel may reach another device: no remote copies, remote signals or barrier semaphores. Data moves between devices by JAX's collectives and lax.ppermute only.
A program may use at most 128 MiB of HBM per device.

```python
import jax
import jax.numpy as jnp
from jax import lax

H = 1792
TOK_DEV = 512
V = 9728
TOKENS = 4096


def base_weight(key):
    key = jax.random.fold_in(key, 71)
    scale_key, value_key = jax.random.split(key)
    column_scale = jnp.exp(jax.random.uniform(scale_key, (V,), jnp.float32, jnp.log(0.5), jnp.log(3.0)))
    values = jax.random.normal(value_key, (H, V), jnp.float32)
    return values * H ** (-0.5) * column_scale[None, :]


def draw_out_weight(key, part):
    return base_weight(key).astype(jnp.bfloat16)


def draw_hidden(key, part):
    key = jax.random.fold_in(key, 3)
    scale_key, value_key = jax.random.split(key, 2)
    row_scale = jnp.exp(jax.random.uniform(scale_key, (TOKENS,), jnp.float32, jnp.log(0.05), jnp.log(0.3)))
    result = jax.random.normal(value_key, (TOKENS, H), jnp.float32) * row_scale[:, None]
    return result.astype(jnp.bfloat16)


def draw_teacher_logits(key, part):
    key = jax.random.fold_in(key, 5)
    row_key, column_key, value_key = jax.random.split(key, 3)
    row_scale = jnp.exp(jax.random.uniform(row_key, (TOKENS,), jnp.float32, jnp.log(1.0), jnp.log(4.0)))
    column_scale = jnp.exp(jax.random.uniform(column_key, (V,), jnp.float32, jnp.log(0.8), jnp.log(3.0)))
    result = jax.random.normal(value_key, (TOKENS, V), jnp.float32) * row_scale[:, None] * column_scale[None, :]
    return result.astype(jnp.bfloat16)


def draw_loss_mask(key, part):
    key = jax.random.fold_in(key, 9)
    draws = jax.random.randint(key, (TOKENS,), 0, 1000)
    threshold = 250 + 650 * jnp.arange(TOKENS) // TOKENS
    return (draws < threshold).astype(jnp.int32)


def touch_ends(values, own_key, low, top_value):
    place = [jax.random.randint(jax.random.fold_in(own_key, axis), (), 0, length) for axis, length in enumerate(values.shape)]
    longest = values.shape.index(max(values.shape))
    neighbour = place[:longest] + [(place[longest] + 1) % values.shape[longest]] + place[longest + 1:]
    return values.at[tuple(place)].set(low).at[tuple(neighbour)].set(top_value)


def setup_inputs(seed: int = 0) -> dict:
    splits = jax.random.split(jax.random.key(seed), 6)
    hidden = draw_hidden(jax.random.fold_in(splits[5], 71), 0)
    out_weight = draw_out_weight(jax.random.fold_in(splits[5], 71), 0)
    teacher_logits = draw_teacher_logits(jax.random.fold_in(splits[5], 71), 0)
    token_ids = touch_ends(jax.random.randint(splits[3], (TOKENS,), 0, V), jax.random.fold_in(splits[3], 1), 0, V - 1).astype(jnp.int32)
    loss_mask = draw_loss_mask(jax.random.fold_in(splits[5], 71), 0)
    return {"hidden": hidden, "out_weight": out_weight, "teacher_logits": teacher_logits, "token_ids": token_ids, "loss_mask": loss_mask}


def reference(hidden, out_weight, teacher_logits, token_ids, loss_mask):
    teacher_all = jnp.roll(teacher_logits, TOKENS // 2, axis=0)
    mask_all = loss_mask.astype(jnp.float32)
    mask_total = jnp.maximum(jnp.sum(mask_all), 1.0)
    blocks = TOKENS // TOK_DEV
    hidden_blocks = hidden.reshape(blocks, TOK_DEV, H)
    teacher_blocks = teacher_all.reshape(blocks, TOK_DEV, V)
    id_blocks = token_ids.reshape(blocks, TOK_DEV)
    mask_blocks = mask_all.reshape(blocks, TOK_DEV)

    def step(weight_sum, inputs):
        rows, teacher_rows, ids_rows, mask_rows = inputs
        logits = jnp.dot(rows, out_weight, preferred_element_type=jnp.float32)
        teacher = teacher_rows.astype(jnp.float32)
        lse_student = jax.nn.logsumexp(logits, axis=1)
        lse_teacher = jax.nn.logsumexp(teacher, axis=1)
        log_student = logits - lse_student[:, None]
        log_teacher = teacher - lse_teacher[:, None]
        probs = jnp.exp(log_student)
        gap = log_student - log_teacher
        kl_rows = jnp.sum(probs * gap, axis=1)
        chosen = jnp.take_along_axis(log_student, ids_rows[:, None].astype(jnp.int32), axis=1)[:, 0]
        grad_logits = ((mask_rows / mask_total)[:, None] * probs * (gap - kl_rows[:, None])).astype(jnp.bfloat16)
        grad_rows = lax.dot_general(grad_logits, out_weight, (((1,), (1,)), ((), ())), preferred_element_type=jnp.float32).astype(jnp.bfloat16)
        weight_sum = weight_sum + lax.dot_general(rows, grad_logits, (((0,), (0,)), ((), ())), preferred_element_type=jnp.float32)
        return weight_sum, (kl_rows, chosen, grad_rows)

    weight_sum, outputs = lax.scan(step, jnp.zeros((H, V), jnp.float32), (hidden_blocks, teacher_blocks, id_blocks, mask_blocks))
    kl_rows, chosen, grad_rows = outputs
    return kl_rows.reshape(TOKENS), chosen.reshape(TOKENS), grad_rows.reshape(TOKENS, H), weight_sum.astype(jnp.bfloat16)
```

```python
import functools

import jax
import jax.numpy as jnp
from jax import lax
from jax.experimental import pallas as pl
from jax.experimental.pallas import tpu as pltpu
from jax.sharding import PartitionSpec as P

F32 = jnp.float32
BF16 = jnp.bfloat16
VMEM_LIMIT = 18 * 1024 * 1024
LANES = 128
STEP = 16
LONG = 20_000_000_000
COST = 2_000_000_000
DIGIT = 128
STATS = 8
QUARTERS = 4


def exchange(array, axes, size, partner):
    return lax.ppermute(array, axes, [(i, partner(i)) for i in range(size)])


def xor_swap(array, axis, mask):
    return exchange(array, axis, lax.axis_size(axis), lambda i: i ^ mask)


def shape(dims, dtype):
    return jax.ShapeDtypeStruct(dims, dtype)


def call(kernel, name, outs, arrays, scratch=(), after=(), far=(), aliases=False, flops=1024):
    skip = len(after)
    on_chip = pl.BlockSpec(memory_space=pltpu.VMEM)
    in_hbm = pl.BlockSpec(memory_space=pltpu.HBM)
    return pl.pallas_call(
        lambda *refs: kernel(*refs[skip:]),
        in_specs=[pl.BlockSpec(memory_space=pl.ANY)] * (skip + len(far))
        + [on_chip] * len(arrays),
        out_specs=[on_chip if isinstance(o, jax.ShapeDtypeStruct) else in_hbm for o in outs],
        out_shape=outs,
        scratch_shapes=list(scratch),
        input_output_aliases={skip: 0} if aliases else {},
        compiler_params=pltpu.CompilerParams(vmem_limit_bytes=VMEM_LIMIT),
        cost_estimate=pl.CostEstimate(flops=flops, bytes_accessed=1024, transcendentals=0),
        name=name,
    )(*after, *far, *arrays)


def column_chunks(width, shares):
    bounds = [width // LANES * sum(shares[:i]) // sum(shares) for i in range(len(shares) + 1)]
    return [(a * LANES, (b - a) * LANES) for a, b in zip(bounds, bounds[1:])]


def tiles(start, size, step):
    return [(at, min(step, start + size - at)) for at in range(start, start + size, step)]


def spread(row):
    return jnp.broadcast_to(row, (LANES, row.shape[1])).T


def lane_sum(ref):
    return jnp.sum(ref[...].T, axis=0, keepdims=True)


def fold(row):
    return jnp.concatenate([row[:, at : at + LANES] for at in range(0, row.shape[1], LANES)])


def unfold(values, k, count):
    each = count // LANES
    rows = [values[k * each + i : k * each + i + 1] for i in range(each)]
    return jnp.concatenate(rows, axis=1)


def pad_rows(values, rows):
    return jnp.concatenate([values, jnp.zeros((rows - values.shape[0], LANES), values.dtype)])


def row_steps(total, group):
    block = total // QUARTERS
    inside = block // 2

    def at(i):
        quarter, rest = i * STEP // inside, i * STEP % inside
        here = pl.multiple_of(i * STEP, STEP)
        there = pl.multiple_of(quarter * block + group * inside + rest, STEP)
        return pl.ds(here, STEP), pl.ds(there, STEP)

    return at


def copy_pairs(source, target, parts=4):
    rows = source.shape[0]
    size = max(STEP, -(-rows // parts) // STEP * STEP)
    return [
        (source.at[at : min(at + size, rows), :], target.at[at : min(at + size, rows), :])
        for at in range(0, rows, size)
    ]


def run_copies(pairs, done):
    copies = [pltpu.make_async_copy(*pair, done.at[i]) for i, pair in enumerate(pairs)]
    for copy in copies:
        copy.start()
    for copy in copies:
        copy.wait()


def near_of(index):
    return index ^ (2 if index & 1 else 4)


def far_of(index):
    return index ^ (4 if index & 1 else 2)


def weight_order():
    me = lax.axis_index("role") * 4 + lax.axis_index("dp")
    order = []
    for index in (me ^ 1, me):
        near = 4 - 2 * (index & 1)
        far = 6 - near
        order += [index ^ near ^ far, index ^ near, index ^ far, index]
    return order


def hidden_order(vocab_size):
    order = [lax.axis_index("vocab")]
    bit = vocab_size // 2
    while bit:
        order = [o ^ bit for o in order] + order
        bit //= 2
    return order


def pick_kernel(hidden, *refs, pieces, extra):
    sources, refs = refs[:extra], refs[extra:]
    outs, refs = refs[: len(pieces)], refs[len(pieces) :]
    landed, done = refs[:-1], refs[-1]
    odd = lax.axis_index("vocab") & 1
    block = hidden.shape[0] // QUARTERS
    size = block // 2
    pairs = list(zip(sources, landed))
    for (group, k), out in zip(pieces, outs):
        at = pl.multiple_of((2 * odd + k) * block + group * size, size)
        pairs += copy_pairs(hidden.at[pl.ds(at, size), :], out.at[:, : hidden.shape[1]])
    run_copies(pairs, done)
    if extra:
        ids, mask = (ref[...] for ref in landed)
        rest, terms = ids, []
        for _ in range(3):
            terms.append(rest & (DIGIT - 1))
            rest = rest >> (DIGIT.bit_length() - 1)
        values = jnp.concatenate([fold(v) for v in (*terms, mask)])
        outs[0][:, outs[0].shape[1] - LANES :] = pad_rows(values.astype(F32), size).astype(BF16)


def pick_rows(hidden, pieces, extra=(), after=()):
    rows, features = hidden.shape
    size = rows // QUARTERS // 2
    far = [pltpu.with_memory_space_constraint(a, pltpu.HBM) for a in (hidden, *extra)]
    more = [LANES if extra and i == 0 else 0 for i in range(len(pieces))]
    return call(
        functools.partial(pick_kernel, pieces=pieces, extra=len(extra)),
        "pick_rows",
        [shape((size, features + n), BF16) for n in more],
        [],
        [pltpu.VMEM((1, rows), jnp.int32)] * len(extra)
        + [pltpu.SemaphoreType.DMA((4 * len(pieces) + len(extra),))],
        after,
        far,
        flops=LONG,
    )


def unpack_kernel(packed, piece, side):
    features, count = piece.shape[1], side.shape[1]
    piece[...] = packed[:, :features]
    values = packed[:, features:].astype(F32)
    digits = [unfold(values, k, count) for k in range(4)]
    side[0:1, :] = digits[0] + DIGIT * (digits[1] + DIGIT * digits[2])
    side[1:2, :] = digits[3]


def unpack_rows(packed, rows):
    dims = (packed.shape[0], packed.shape[1] - LANES)
    return call(
        unpack_kernel,
        "unpack_rows",
        [shape(dims, BF16), shape((2, rows), F32)],
        [packed],
    )


def teacher_kernel(teacher, out, top, total):
    rows, width = teacher.shape

    @pl.loop(0, rows // STEP, unroll=2)
    def _(i):
        at = pl.ds(pl.multiple_of(i * STEP, STEP), STEP)
        best = teacher[at, 0:LANES]
        for start, size in tiles(LANES, width - LANES, LANES):
            best = jnp.maximum(best, teacher[at, start : start + size])
        top[at, :] = best.astype(F32)

    top_row = jnp.max(top[...].T, axis=0, keepdims=True)
    top[...] = spread(top_row)

    @pl.loop(0, rows // STEP, unroll=2)
    def _(i):
        at = pl.ds(pl.multiple_of(i * STEP, STEP), STEP)
        shift = top[at, :]
        acc = jnp.zeros((STEP, LANES), F32)
        for start, size in tiles(0, width, LANES):
            acc += jnp.exp(teacher[at, start : start + size].astype(F32) - shift)
        total[at, :] = acc

    out[...] = jnp.concatenate(
        [jnp.zeros((3, rows), F32), top_row, lane_sum(total), jnp.zeros((3, rows), F32)]
    )


def teacher_stats(teacher, after=()):
    rows, width = teacher.shape
    return call(
        teacher_kernel,
        "teacher_stats",
        [shape((STATS, rows), F32)],
        [teacher],
        [pltpu.VMEM((rows, LANES), F32)] * 2,
        after,
        flops=LONG,
    )[0]


def pass_on(array, after):
    outs = [shape(array.shape, array.dtype)]
    return call(lambda *refs: None, "pass_on", outs, [], (), after, [array], True)[0]


def count_kernel(side, mask, out):
    total = jnp.sum(side[1:2, :]) + jnp.sum(mask[...].astype(F32))
    out[...] = jnp.full(out.shape, total)


def sum_kernel(first, second, out):
    out[...] = first[...] + second[...]


def count_rows(side, mask):
    return call(count_kernel, "count_rows", [shape((8, LANES), F32)], [side, mask])[0]


def sum_rows(first, second):
    return call(sum_kernel, "sum_rows", [shape((8, LANES), F32)], [first, second])[0]


def gather_rows(direct, other, rows_in):
    odd = lax.axis_index("vocab") & 1
    half = rows_in.shape[0] // 2
    for first, refs in ((odd, direct), (1 - odd, other)):
        for i, ref in enumerate(refs):
            count = ref.shape[0]
            at = pl.multiple_of(first * half + i * count, count)
            rows_in[pl.ds(at, count), :] = ref[...]


def turn_rows(direct, other, after=()):
    count = len(direct)
    rows, features = 2 * count * direct[0].shape[0], direct[0].shape[1]

    def kernel(*refs):
        out, rows_in, turned = refs[2 * count :]
        gather_rows(refs[:count], refs[count : 2 * count], rows_in)
        turned[...] = rows_in[...].T
        height = features // 8
        for i, block in enumerate(weight_order()):
            at = pl.ds(pl.multiple_of(block * height, STEP), height)
            out[i * height : (i + 1) * height, :] = turned[at, :]

    return call(
        kernel,
        "turn_rows",
        [shape((features, rows), BF16)],
        [*direct, *other],
        [pltpu.VMEM((rows, features), BF16), pltpu.VMEM((features, rows), BF16)],
        after,
    )[0]


def logits_kernel(direct, other, weight, teacher, side, known, *refs):
    group = len(refs) - 8
    first, refs = refs[:group], refs[group:]
    logits, stats, rows_in, top, total, gap, picked, chosen = refs
    rows, width = logits.shape
    vocab = lax.axis_index("vocab")
    gather_rows(direct, other, rows_in)
    value = rows_in[...]

    best = None
    for start, size in tiles(0, width, 2 * LANES):
        tile = jnp.dot(value, weight[:, start : start + size], preferred_element_type=F32)
        logits[:, start : start + size] = tile
        for at in range(0, size, LANES):
            part = tile[:, at : at + LANES]
            best = part if best is None else jnp.maximum(best, part)
    top[...] = spread(jnp.max(best.T, axis=0, keepdims=True))

    ids = side[0:1, :] - (vocab * width).astype(F32)
    chosen[...] = spread(ids) - lax.broadcasted_iota(
        jnp.int32, chosen.shape, 1
    ).astype(F32)
    steps = row_steps(2 * rows, group)
    for ref in (total, gap, picked):
        ref[...] = jnp.zeros(ref.shape, F32)

    @pl.loop(0, rows // STEP, unroll=2)
    def _(i):
        here, there = steps(i)
        shift, wanted = top[here, :], chosen[there, :]
        sums = [jnp.zeros((STEP, LANES), F32)] * 3
        for start, size in tiles(0, width, LANES):
            student = logits[here, start : start + size]
            target = teacher[there, start : start + size].astype(F32)
            share = jnp.exp(student - shift)
            sums[0] += share
            sums[1] += share * (student - target)
            sums[2] += jnp.where(wanted == start, student, 0.0)
        total[there, :], gap[there, :], picked[there, :] = sums

    rows_known = {k: lane_sum(ref) for k, ref in ((1, total), (2, gap), (5, picked))}
    inside = rows // QUARTERS
    for q in range(QUARTERS):
        at = (2 * q + group) * inside
        total[at : at + inside, :] = top[q * inside : (q + 1) * inside, :]
    rows_known[0] = total[...].T[0:1, :]
    stats[...] = known[...]
    for k, row in rows_known.items():
        if first:
            lane = lax.broadcasted_iota(jnp.int32, row.shape, 1)
            row = jnp.where((lane & inside) != 0, row, first[0][k : k + 1, :])
        stats[k : k + 1, :] = row


def group_logits(direct, other, weight, teacher, side, known, first, after=()):
    rows, width = teacher.shape
    features = weight.shape[0]
    count = len(direct)

    def kernel(*refs):
        logits_kernel(refs[:count], refs[count : 2 * count], *refs[2 * count :])

    return call(
        kernel,
        "group_logits",
        [
            shape((rows // 2, width), F32),
            shape((STATS, rows), F32),
        ],
        [*direct, *other, weight, teacher, side, known, *first],
        [pltpu.VMEM((rows // 2, features), BF16)]
        + [pltpu.VMEM((rows // 2, LANES), F32)]
        + [pltpu.VMEM((rows, LANES), F32)] * 4,
        after,
        flops=LONG if first else COST,
    )


def join(parts):
    top = functools.reduce(jnp.maximum, [p[0] for p in parts])
    teacher_top = functools.reduce(jnp.maximum, [p[3] for p in parts])
    scales = [jnp.exp(p[0] - top) for p in parts]
    total = sum(s * p[1] for s, p in zip(scales, parts))
    gap = sum(s * p[2] for s, p in zip(scales, parts))
    teacher_total = sum(jnp.exp(p[3] - teacher_top) * p[4] for p in parts)
    picked = sum(p[5] for p in parts)
    return top, total, gap, teacher_top, teacher_total, picked


def over_vocab(stats, size):
    parts, done = [stats], 1
    while done < size:
        if done > 1:
            joined = join([[p[k] for k in range(6)] for p in parts])
            parts = [jnp.stack(list(joined) + [joined[0]] * (STATS - 6))]
        radix = min(4, size // done)
        parts += [xor_swap(parts[0], "vocab", k * done) for k in reversed(range(1, radix))]
        done *= radix
    return parts


def slope_kernel(*refs, parts):
    stats = refs[:parts]
    side, *counts, teacher, logits_0, logits_1 = refs[parts : parts + 6]
    slope_0, slope_1, tokens, lses, shifts, weights = refs[parts + 6 :]

    top, total, gap, teacher_top, teacher_total, picked = join(
        [[s[k : k + 1, :] for k in range(6)] for s in stats]
    )
    lse = top + jnp.log(total)
    diff = lse - (teacher_top + jnp.log(teacher_total))
    kl = gap / total - diff
    tokens[...] = jnp.concatenate([kl, picked - lse])
    mask_total = counts[0][0:1, 0:1] + counts[1][0:1, 0:1]
    lses[...] = spread(lse)
    shifts[...] = spread(diff + kl)
    weights[...] = spread(side[1:2, :] / jnp.maximum(mask_total, 1.0))
    for group, (logits, slope) in enumerate(((logits_0, slope_0), (logits_1, slope_1))):
        rows, width = logits.shape
        steps = row_steps(2 * rows, group)

        @pl.loop(0, rows // STEP, unroll=2)
        def _(i):
            here, there = steps(i)
            lse, shift, weight = lses[there, :], shifts[there, :], weights[there, :]
            for start, size in tiles(0, width, LANES):
                student = logits[here, start : start + size]
                target = teacher[there, start : start + size].astype(F32)
                value = weight * jnp.exp(student - lse) * (student - target - shift)
                slope[here, start : start + size] = value.astype(BF16)


def slopes_of(stats, side, counts, teacher, logits, after=()):
    rows, width = teacher.shape
    return call(
        functools.partial(slope_kernel, parts=len(stats)),
        "slopes",
        [shape((rows // 2, width), BF16)] * 2 + [shape((2, rows), F32)],
        [*stats, side, *counts, teacher, *logits],
        [pltpu.VMEM((rows, LANES), F32)] * 3,
        after,
    )


def weight_blocks(hidden_t, slopes, first, count, start, size):
    return sum(
        jnp.dot(
            left[first : first + count, :],
            right[:, start : start + size],
            preferred_element_type=F32,
        )
        for left, right in zip(hidden_t, slopes)
    )


def weight_away_kernel(*refs, start):
    hidden_t, slopes, out = refs[:2], refs[2:4], refs[4]
    out[...] = weight_blocks(hidden_t, slopes, 0, out.shape[0], start, out.shape[1]).astype(BF16)


def weight_away(hidden_t, slopes, start, size, after=()):
    features = hidden_t[0].shape[0]
    return call(
        functools.partial(weight_away_kernel, start=start),
        "weight_away",
        [shape((features // 2, size), BF16)],
        [*hidden_t, *slopes],
        (),
        after,
    )[0]


def weight_home_kernel(*refs, start):
    hidden_t, slopes, received, outs = refs[:2], refs[2:4], refs[4], refs[5:]
    count, size = outs[0].shape
    for part, out in enumerate(outs):
        value = weight_blocks(hidden_t, slopes, (2 + part) * count, count, start, size)
        value += received[part * count : (part + 1) * count, :].astype(F32)
        out[...] = value.astype(BF16)


def weight_home(hidden_t, slopes, received, start, after=()):
    count, size = received.shape
    return call(
        functools.partial(weight_home_kernel, start=start),
        "weight_home",
        [shape((count // 2, size), BF16)] * 2,
        [*hidden_t, *slopes, received],
        (),
        after,
    )


def hidden_kernel(*refs, vocab_size):
    *slopes, weight, away, home, rows = refs
    blocks = vocab_size
    height = rows.shape[0] // blocks
    for i, block in enumerate(hidden_order(vocab_size)):
        to = slice(i * height, (i + 1) * height)
        if len(slopes) == 1:
            rows[to, :] = slopes[0][pl.ds(pl.multiple_of(block * height, height), height), :]
        else:
            per = vocab_size // QUARTERS // 2
            at = (block // (2 * per) * per + block % per) * height
            for group, slope in enumerate(slopes):

                @pl.when(block // per % 2 == group)
                def _():
                    rows[to, :] = slope[pl.ds(pl.multiple_of(at, height), height), :]

    value = rows[...]
    middle = away.shape[0]
    for start, size in tiles(0, weight.shape[0], 2 * LANES):
        at = slice(start, start + size)
        result = lax.dot_general(
            value, weight[at, :], (((1,), (1,)), ((), ())), preferred_element_type=F32
        )
        away[:, at] = result[:middle].astype(BF16)
        home[:, at] = result[middle:]


def hidden_blocks(slopes, weight, vocab_size, after=()):
    width = weight.shape[1]
    rows = sum(s.shape[0] for s in slopes)
    dims = (rows // 2, weight.shape[0])
    return call(
        functools.partial(hidden_kernel, vocab_size=vocab_size),
        "hidden_grad",
        [shape(dims, BF16), shape(dims, F32)],
        [*slopes, weight],
        [pltpu.VMEM((rows, width), BF16)],
        after,
    )


def add_kernel(kept, received, *outs):
    count = outs[0].shape[0]
    for i, out in enumerate(outs):
        at = slice(i * count, (i + 1) * count)
        out[...] = (kept[at, :].astype(F32) + received[at, :].astype(F32)).astype(BF16)


def add(kept, received, parts, after=()):
    rows, width = kept.shape
    return call(
        add_kernel,
        "add",
        [shape((rows // parts, width), BF16)] * parts,
        [kept, received],
        (),
        after,
    )


def pack_kernel(kept, received, tokens, out):
    rows, width = kept.shape
    out[:, :width] = (kept[...].astype(F32) + received[...].astype(F32)).astype(BF16)
    rest, terms = tokens[...], []
    for _ in range(3):
        terms.append(rest.astype(BF16).astype(F32))
        rest = rest - terms[-1]
    rows_of = [fold(term[k : k + 1]) for term in terms for k in range(2)]
    room = rows * (out.shape[1] - width) // LANES
    values = pad_rows(jnp.concatenate(rows_of), room).astype(BF16)
    for i in range(room // rows):
        at = width + i * LANES
        out[:, at : at + LANES] = values[i * rows : (i + 1) * rows]


def pack(kept, received, tokens, after=()):
    rows, width = kept.shape
    need = 6 * tokens.shape[1] // LANES
    outs = [shape((rows, width + -(-need // rows) * LANES), BF16)]
    return call(pack_kernel, "pack", outs, [kept, received, tokens], (), after)


def finish_kernel(*refs, start, so_far, tokens):
    refs = refs[so_far:]
    if tokens:
        strip, out, token, *values, done = refs
        count, width = strip.shape[0], out.shape[1]
        folded = jnp.concatenate(
            [strip[:, at : at + LANES] for at in range(width, strip.shape[1], LANES)]
        ).astype(F32)
        for k, value in enumerate(values):
            size = value.shape[1]
            value[...] = sum(unfold(folded, k + 2 * term, size) for term in range(3))
        source, place = strip.at[:, :width], out.at[start : start + count, :]
    elif len(refs) == 4:
        strip, out, token, done = refs
        count = strip.shape[0]
        source, place = strip, out.at[start : start + count, :]
    else:
        kept, received, out, token, source, done = refs
        source[...] = (kept[...].astype(F32) + received[...].astype(F32)).astype(BF16)
        place = out.at[:, start : start + source.shape[1]]
    token[...] = jnp.zeros(token.shape, F32)
    run_copies(copy_pairs(source, place), done)


def finish(parts, dims, start, so_far, after, tokens=0):
    outs = [pltpu.HBM(dims, BF16), shape((8, LANES), F32)]
    outs += [shape((1, tokens), F32)] * 2 if tokens else []
    scratch = [pltpu.VMEM(parts[0].shape, BF16)] if len(parts) == 2 else []
    return call(
        functools.partial(
            finish_kernel, start=start, so_far=len(so_far), tokens=bool(tokens)
        ),
        "finish",
        outs,
        list(parts),
        scratch + [pltpu.SemaphoreType.DMA((8,))],
        after,
        so_far,
        bool(so_far),
    )


def local(hidden, out_weight, teacher_logits, token_ids, loss_mask):
    rows, features = hidden.shape
    width = out_weight.shape[1]
    vocab_size = lax.axis_size("vocab")
    group_axes, group_size = ("role", "dp"), lax.axis_size("role") * lax.axis_size("dp")
    assert lax.axis_size("role") == 2 and lax.axis_size("dp") == 4
    assert vocab_size & (vocab_size - 1) == 0 and vocab_size >= QUARTERS

    ids, mask = token_ids.reshape(1, rows), loss_mask.reshape(1, rows)
    pieces = list(pick_rows(hidden, [(0, 0)]))
    pieces += pick_rows(hidden, [(0, 1), (1, 0), (1, 1)], (ids, mask), after=pieces)
    direct = [xor_swap(piece, "role", 1) for piece in pieces]
    known = teacher_stats(teacher_logits, after=pieces[1:2])
    direct[0] = pass_on(direct[0], [known])
    direct[1], side = unpack_rows(direct[1], rows)
    count = count_rows(side, mask)
    count = sum_rows(count, xor_swap(count, "dp", 1))
    direct[2] = pass_on(direct[2], [count])
    counts = [count, xor_swap(count, "dp", 2)]
    other = [xor_swap(piece, "vocab", 1) for piece in direct]

    logits, hidden_t, stats = [], [], []
    for group in range(2):
        pair = slice(2 * group, 2 * group + 2)
        done = group_logits(
            direct[pair],
            other[pair],
            out_weight,
            teacher_logits,
            side,
            known,
            stats[-1:],
            after=counts[1:] if group else direct[3:],
        )
        for values, value in zip((logits, stats), done):
            values.append(value)
        hidden_t.append(turn_rows(direct[pair], other[pair], after=stats[group:]))
    *slopes, tokens = slopes_of(
        over_vocab(stats[1], vocab_size), side, counts, teacher_logits, logits, hidden_t[1:]
    )

    parts = [[s] for s in slopes] if vocab_size == QUARTERS else [slopes]
    home, hidden_in = [], []

    def hidden_step(last):
        if len(home) < len(parts):
            some = parts[len(home)]
            last, kept = hidden_blocks(some, out_weight, vocab_size, after=[last])
            home.append(kept)
            hidden_in.append(xor_swap(last, "vocab", 1))
        return last

    chunks = column_chunks(width, (7, 6, 6))
    arrived, near = [], []

    def away_step(last):
        last = weight_away(hidden_t, slopes, *chunks[len(arrived)], after=[last])
        arrived.append(exchange(last, group_axes, group_size, lambda i: i ^ 1))
        return last

    def near_step(last):
        k = len(near)
        leaving, last = weight_home(hidden_t, slopes, arrived[k], chunks[k][0], after=[last])
        near.append((last, exchange(leaving, group_axes, group_size, near_of)))
        return last

    far, grad_weight, grad_hidden, returned, outs = [], [], [], [], []

    def far_step(last):
        kept, received = near[len(far)]
        leaving, last = add(kept, received, 2, after=[last])
        far.append((last, exchange(leaving, group_axes, group_size, far_of)))
        return last

    def weight_step(last):
        k = len(grad_weight)
        dims = (features // group_size, width)
        result, last = finish(far[k], dims, chunks[k][0], grad_weight[-1:], [last])
        grad_weight.append(result)
        return last

    halved = []

    def halve_step(last):
        if len(halved) < len(home):
            k = len(halved)
            leaving, last = add(home[k], hidden_in[k], 2, after=[last])
            halved.append((last, xor_swap(leaving, "vocab", 2)))
        return last

    def return_step(last):
        if len(returned) < len(home):
            kept, received = halved[len(returned)]
            bit = 4
            while bit < vocab_size:
                leaving, last = add(kept, received, 2, after=[last])
                kept, received = last, xor_swap(leaving, "vocab", bit)
                bit *= 2
            if returned:
                (last,) = add(kept, received, 1, after=[last])
            else:
                (last,) = pack(kept, received, tokens, after=[last])
            returned.append(xor_swap(last, "role", 1))
        return last

    def strip_step(last):
        if len(grad_hidden) < len(home):
            k = len(grad_hidden)
            strip = returned[k]
            dims = (rows // vocab_size, features)
            start = k * strip.shape[0] if k == 0 else dims[0] // 2
            result, last, *values = finish(
                [strip], dims, start, grad_hidden[-1:], [last], 0 if k else rows
            )
            grad_hidden.append(result)
            outs.extend(values)
        return last

    last = slopes[1]
    for step in (
        away_step,
        away_step,
        away_step,
        near_step,
        hidden_step,
        near_step,
        near_step,
        hidden_step,
        far_step,
        halve_step,
        far_step,
        halve_step,
        return_step,
        weight_step,
        far_step,
        weight_step,
        return_step,
        strip_step,
        weight_step,
        strip_step,
    ):
        last = step(last)

    return outs[0].reshape(rows), outs[1].reshape(rows), grad_hidden[-1], grad_weight[-1]


def solution(mesh):
    return jax.shard_map(
        local,
        mesh=mesh,
        in_specs=(
            P(("role", "dp"), None),
            P(None, "vocab"),
            P(("role", "dp"), "vocab"),
            P(("role", "dp")),
            P(("role", "dp")),
        ),
        out_specs=(
            P(("role", "dp")),
            P(("role", "dp")),
            P(("role", "dp", "vocab"), None),
            P(("role", "dp"), "vocab"),
        ),
        check_vma=False,
    )
```

```python
import functools

import jax
import jax.numpy as jnp
from jax import lax
from jax.experimental import pallas as pl
from jax.experimental.pallas import tpu as pltpu
from jax.sharding import PartitionSpec as P

F32 = jnp.float32
BF16 = jnp.bfloat16
VMEM_LIMIT = 18 * 1024 * 1024
LANES = 128
STEP = 16
LONG = 20_000_000_000
COST = 2_000_000_000
DIGIT = 128
BAND = 32
STATS = 8
QUARTERS = 4


def exchange(array, axes, size, partner):
    return lax.ppermute(array, axes, [(i, partner(i)) for i in range(size)])


def xor_swap(array, axis, mask):
    return exchange(array, axis, lax.axis_size(axis), lambda i: i ^ mask)


def shape(dims, dtype):
    return jax.ShapeDtypeStruct(dims, dtype)


def call(kernel, name, outs, arrays, scratch=(), after=(), far=(), aliases=False, flops=1024):
    skip = len(after)
    on_chip = pl.BlockSpec(memory_space=pltpu.VMEM)
    in_hbm = pl.BlockSpec(memory_space=pltpu.HBM)
    return pl.pallas_call(
        lambda *refs: kernel(*refs[skip:]),
        in_specs=[pl.BlockSpec(memory_space=pl.ANY)] * (skip + len(far))
        + [on_chip] * len(arrays),
        out_specs=[on_chip if isinstance(o, jax.ShapeDtypeStruct) else in_hbm for o in outs],
        out_shape=outs,
        scratch_shapes=list(scratch),
        input_output_aliases={skip: 0} if aliases else {},
        compiler_params=pltpu.CompilerParams(vmem_limit_bytes=VMEM_LIMIT),
        cost_estimate=pl.CostEstimate(flops=flops, bytes_accessed=1024, transcendentals=0),
        name=name,
    )(*after, *far, *arrays)


def column_chunks(width, shares):
    bounds = [width // LANES * sum(shares[:i]) // sum(shares) for i in range(len(shares) + 1)]
    return [(a * LANES, (b - a) * LANES) for a, b in zip(bounds, bounds[1:])]


def tiles(start, size, step):
    return [(at, min(step, start + size - at)) for at in range(start, start + size, step)]


def spread(row):
    return jnp.broadcast_to(row, (LANES, row.shape[1])).T


def lane_sum(ref):
    return jnp.sum(ref[...].T, axis=0, keepdims=True)


def fold(row):
    return jnp.concatenate([row[:, at : at + LANES] for at in range(0, row.shape[1], LANES)])


def unfold(values, k, count):
    each = count // LANES
    rows = [values[k * each + i : k * each + i + 1] for i in range(each)]
    return jnp.concatenate(rows, axis=1)


def pad_rows(values, rows):
    return jnp.concatenate([values, jnp.zeros((rows - values.shape[0], LANES), values.dtype)])


def row_steps(total, group):
    block = total // QUARTERS
    inside = block // 2

    def at(i):
        quarter, rest = i * STEP // inside, i * STEP % inside
        here = pl.multiple_of(i * STEP, STEP)
        there = pl.multiple_of(quarter * block + group * inside + rest, STEP)
        return pl.ds(here, STEP), pl.ds(there, STEP)

    return at


def copy_pairs(source, target, parts=4):
    rows = source.shape[0]
    size = max(STEP, -(-rows // parts) // STEP * STEP)
    return [
        (source.at[at : min(at + size, rows), :], target.at[at : min(at + size, rows), :])
        for at in range(0, rows, size)
    ]


def run_copies(pairs, done):
    copies = [pltpu.make_async_copy(*pair, done.at[i]) for i, pair in enumerate(pairs)]
    for copy in copies:
        copy.start()
    for copy in copies:
        copy.wait()


def near_of(index):
    return index ^ (2 if index & 1 else 4)


def far_of(index):
    return index ^ (4 if index & 1 else 2)


def weight_order():
    me = lax.axis_index("role") * 4 + lax.axis_index("dp")
    order = []
    for index in (me ^ 1, me):
        near = 4 - 2 * (index & 1)
        far = 6 - near
        order += [index ^ near ^ far, index ^ near, index ^ far, index]
    return order


def hidden_order(vocab_size):
    order = [lax.axis_index("vocab")]
    bit = vocab_size // 2
    while bit:
        order = [o ^ bit for o in order] + order
        bit //= 2
    return order


def pick_kernel(hidden, *refs, pieces, extra):
    sources, refs = refs[:extra], refs[extra:]
    outs, refs = refs[: len(pieces)], refs[len(pieces) :]
    landed, done = refs[:-1], refs[-1]
    odd = lax.axis_index("vocab") & 1
    block = hidden.shape[0] // QUARTERS
    size = block // 2
    pairs = list(zip(sources, landed))
    for (group, k), out in zip(pieces, outs):
        at = pl.multiple_of((2 * odd + k) * block + group * size, size)
        pairs += copy_pairs(hidden.at[pl.ds(at, size), :], out.at[:, : hidden.shape[1]])
    run_copies(pairs, done)
    if extra:
        ids, mask = (ref[...] for ref in landed)
        rest, terms = ids, []
        for _ in range(3):
            terms.append(rest & (DIGIT - 1))
            rest = rest >> (DIGIT.bit_length() - 1)
        values = jnp.concatenate([fold(v) for v in (*terms, mask)])
        outs[0][:, outs[0].shape[1] - LANES :] = pad_rows(values.astype(F32), size).astype(BF16)


def pick_rows(hidden, pieces, extra=(), after=()):
    rows, features = hidden.shape
    size = rows // QUARTERS // 2
    far = [pltpu.with_memory_space_constraint(a, pltpu.HBM) for a in (hidden, *extra)]
    more = [LANES if extra and i == 0 else 0 for i in range(len(pieces))]
    return call(
        functools.partial(pick_kernel, pieces=pieces, extra=len(extra)),
        "pick_rows",
        [shape((size, features + n), BF16) for n in more],
        [],
        [pltpu.VMEM((1, rows), jnp.int32)] * len(extra)
        + [pltpu.SemaphoreType.DMA((4 * len(pieces) + len(extra),))],
        after,
        far,
        flops=LONG,
    )


def unpack_kernel(packed, piece, side):
    features, count = piece.shape[1], side.shape[1]
    piece[...] = packed[:, :features]
    values = packed[:, features:].astype(F32)
    digits = [unfold(values, k, count) for k in range(4)]
    side[0:1, :] = digits[0] + DIGIT * (digits[1] + DIGIT * digits[2])
    side[1:2, :] = digits[3]


def unpack_rows(packed, rows):
    dims = (packed.shape[0], packed.shape[1] - LANES)
    return call(
        unpack_kernel,
        "unpack_rows",
        [shape(dims, BF16), shape((2, rows), F32)],
        [packed],
    )


def teacher_kernel(teacher, out, top, total):
    rows, width = teacher.shape

    @pl.loop(0, rows // STEP, unroll=2)
    def _(i):
        at = pl.ds(pl.multiple_of(i * STEP, STEP), STEP)
        best = teacher[at, 0:LANES]
        for start, size in tiles(LANES, width - LANES, LANES):
            best = jnp.maximum(best, teacher[at, start : start + size])
        top[at, :] = best.astype(F32)

    top_row = jnp.max(top[...].T, axis=0, keepdims=True)
    top[...] = spread(top_row)

    @pl.loop(0, rows // STEP, unroll=2)
    def _(i):
        at = pl.ds(pl.multiple_of(i * STEP, STEP), STEP)
        shift = top[at, :]
        acc = jnp.zeros((STEP, LANES), F32)
        for start, size in tiles(0, width, LANES):
            acc += jnp.exp(teacher[at, start : start + size].astype(F32) - shift)
        total[at, :] = acc

    out[...] = jnp.concatenate(
        [jnp.zeros((3, rows), F32), top_row, lane_sum(total), jnp.zeros((3, rows), F32)]
    )


def teacher_stats(teacher, after=()):
    rows, width = teacher.shape
    return call(
        teacher_kernel,
        "teacher_stats",
        [shape((STATS, rows), F32)],
        [teacher],
        [pltpu.VMEM((rows, LANES), F32)] * 2,
        after,
        flops=LONG,
    )[0]


def pass_on(array, after):
    outs = [shape(array.shape, array.dtype)]
    return call(lambda *refs: None, "pass_on", outs, [], (), after, [array], True)[0]


def count_kernel(side, mask, out):
    total = jnp.sum(side[1:2, :]) + jnp.sum(mask[...].astype(F32))
    out[...] = jnp.full(out.shape, total)


def sum_kernel(first, second, out):
    out[...] = first[...] + second[...]


def count_rows(side, mask):
    return call(count_kernel, "count_rows", [shape((8, LANES), F32)], [side, mask])[0]


def sum_rows(first, second):
    return call(sum_kernel, "sum_rows", [shape((8, LANES), F32)], [first, second])[0]


def gather_rows(direct, other, rows_in):
    odd = lax.axis_index("vocab") & 1
    half = rows_in.shape[0] // 2
    for first, refs in ((odd, direct), (1 - odd, other)):
        for i, ref in enumerate(refs):
            count = ref.shape[0]
            at = pl.multiple_of(first * half + i * count, count)
            rows_in[pl.ds(at, count), :] = ref[...]


def turn_rows(direct, other, after=()):
    count = len(direct)
    rows, features = 2 * count * direct[0].shape[0], direct[0].shape[1]

    def kernel(*refs):
        out, rows_in, turned = refs[2 * count :]
        gather_rows(refs[:count], refs[count : 2 * count], rows_in)
        turned[...] = rows_in[...].T
        height = features // 8
        for i, block in enumerate(weight_order()):
            at = pl.ds(pl.multiple_of(block * height, STEP), height)
            out[i * height : (i + 1) * height, :] = turned[at, :]

    return call(
        kernel,
        "turn_rows",
        [shape((features, rows), BF16)],
        [*direct, *other],
        [pltpu.VMEM((rows, features), BF16), pltpu.VMEM((features, rows), BF16)],
        after,
    )[0]


def logits_kernel(direct, other, weight, teacher, side, known, *refs):
    group = len(refs) - 8
    first, refs = refs[:group], refs[group:]
    logits, stats, rows_in, top, total, gap, picked, chosen = refs
    rows, width = logits.shape
    vocab = lax.axis_index("vocab")
    gather_rows(direct, other, rows_in)
    value = rows_in[...]

    ids = side[0:1, :] - (vocab * width).astype(F32)
    chosen[...] = spread(ids) - lax.broadcasted_iota(jnp.int32, chosen.shape, 1).astype(F32)
    for ref in (total, gap, picked):
        ref[...] = jnp.zeros(ref.shape, F32)
    inside = rows // QUARTERS
    for start, size in tiles(0, width, 2 * LANES):
        tile = jnp.dot(value, weight[:, start : start + size], preferred_element_type=F32)
        logits[:, start : start + size] = tile
        columns = range(start, start + size, LANES)
        for at in range(0, rows, BAND):
            here = slice(at, at + BAND)
            from_row = (at // inside * 2 + group) * inside + at % inside
            there = slice(from_row, from_row + BAND)
            students = [tile[here, c - start : c - start + LANES] for c in columns]
            best = functools.reduce(jnp.maximum, students)
            if start:
                last = top[here, :]
                best = jnp.maximum(best, last)
                scale = jnp.exp(last - best)
                sums = [total[there, :] * scale, gap[there, :] * scale]
                hit = picked[there, :]
            else:
                sums, hit = [0.0, 0.0], 0.0
            top[here, :] = best
            wanted = chosen[there, :]
            for c, student in zip(columns, students):
                target = teacher[there, c : c + LANES].astype(F32)
                share = jnp.exp(student - best)
                sums = [sums[0] + share, sums[1] + share * (student - target)]
                hit = hit + jnp.where(wanted == c, student, 0.0)
            total[there, :], gap[there, :], picked[there, :] = *sums, hit

    top_row = jnp.max(top[...].T, axis=0, keepdims=True)
    whole_top = spread(top_row)
    for at in range(0, rows, inside):
        here = slice(at, at + inside)
        from_row = (at // inside * 2 + group) * inside
        there = slice(from_row, from_row + inside)
        scale = jnp.exp(top[here, :] - whole_top[here, :])
        total[there, :] = total[there, :] * scale
        gap[there, :] = gap[there, :] * scale
        top[here, :] = whole_top[here, :]

    rows_known = {k: lane_sum(ref) for k, ref in ((1, total), (2, gap), (5, picked))}
    for q in range(QUARTERS):
        at = (2 * q + group) * inside
        total[at : at + inside, :] = top[q * inside : (q + 1) * inside, :]
    rows_known[0] = total[...].T[0:1, :]
    stats[...] = known[...]
    for k, row in rows_known.items():
        if first:
            lane = lax.broadcasted_iota(jnp.int32, row.shape, 1)
            row = jnp.where((lane & inside) != 0, row, first[0][k : k + 1, :])
        stats[k : k + 1, :] = row


def group_logits(direct, other, weight, teacher, side, known, first, after=()):
    rows, width = teacher.shape
    features = weight.shape[0]
    count = len(direct)

    def kernel(*refs):
        logits_kernel(refs[:count], refs[count : 2 * count], *refs[2 * count :])

    return call(
        kernel,
        "group_logits",
        [
            shape((rows // 2, width), F32),
            shape((STATS, rows), F32),
        ],
        [*direct, *other, weight, teacher, side, known, *first],
        [pltpu.VMEM((rows // 2, features), BF16)]
        + [pltpu.VMEM((rows // 2, LANES), F32)]
        + [pltpu.VMEM((rows, LANES), F32)] * 4,
        after,
        flops=LONG if first else COST,
    )


def join(parts):
    top = functools.reduce(jnp.maximum, [p[0] for p in parts])
    teacher_top = functools.reduce(jnp.maximum, [p[3] for p in parts])
    scales = [jnp.exp(p[0] - top) for p in parts]
    total = sum(s * p[1] for s, p in zip(scales, parts))
    gap = sum(s * p[2] for s, p in zip(scales, parts))
    teacher_total = sum(jnp.exp(p[3] - teacher_top) * p[4] for p in parts)
    picked = sum(p[5] for p in parts)
    return top, total, gap, teacher_top, teacher_total, picked


def join_kernel(first, second, out):
    rows = join([[p[k : k + 1, :] for k in range(6)] for p in (first, second)])
    out[...] = jnp.concatenate([*rows, rows[0], rows[0]])


def over_vocab(stats, size):
    distance = 1
    while distance * 2 < size:
        received = xor_swap(stats, "vocab", distance)
        (stats,) = call(
            join_kernel, "join_stats", [shape(stats.shape, F32)], [stats, received]
        )
        distance *= 2
    return [stats, xor_swap(stats, "vocab", distance)]


def row_kernel(stats, side, counts, tokens, lses, shifts, weights):
    top, total, gap, teacher_top, teacher_total, picked = join(
        [[s[k : k + 1, :] for k in range(6)] for s in stats]
    )
    lse = top + jnp.log(total)
    diff = lse - (teacher_top + jnp.log(teacher_total))
    kl = gap / total - diff
    tokens[...] = jnp.concatenate([kl, picked - lse])
    mask_total = counts[0][0:1, 0:1] + counts[1][0:1, 0:1]
    lses[...] = spread(lse)
    shifts[...] = spread(diff + kl)
    weights[...] = spread(side[1:2, :] / jnp.maximum(mask_total, 1.0))


def slope_kernel(lses, shifts, weights, teacher, *refs, start):
    for group, (logits, slope) in enumerate(zip(refs[:2], refs[2:])):
        rows, width = slope.shape
        steps = row_steps(2 * rows, group)

        @pl.loop(0, rows // STEP, unroll=2)
        def _(i):
            here, there = steps(i)
            lse, shift, weight = lses[there, :], shifts[there, :], weights[there, :]
            for at, size in tiles(0, width, LANES):
                student = logits[here, start + at : start + at + size]
                target = teacher[there, start + at : start + at + size].astype(F32)
                value = weight * jnp.exp(student - lse) * (student - target - shift)
                slope[here, at : at + size] = value.astype(BF16)


def first_slopes(stats, side, counts, teacher, logits, size, after=()):
    rows = teacher.shape[0]
    parts = len(stats)

    def kernel(*refs):
        before, (slope_0, slope_1, *after) = refs[: parts + 6], refs[parts + 6 :]
        side, first, second, teacher, *logits = before[parts:]
        row_kernel(before[:parts], side, (first, second), *after)
        slope_kernel(*after[1:], teacher, *logits, slope_0, slope_1, start=0)

    *slopes, tokens, lses, shifts, weights = call(
        kernel,
        "slopes",
        [shape((rows // 2, size), BF16)] * 2
        + [shape((2, rows), F32)]
        + [shape((rows, LANES), F32)] * 3,
        [*stats, side, *counts, teacher, *logits],
        (),
        after,
    )
    return slopes, tokens, (lses, shifts, weights)


def more_slopes(columns, teacher, logits, start, size, after=()):
    rows = teacher.shape[0]
    return call(
        functools.partial(slope_kernel, start=start),
        "slopes",
        [shape((rows // 2, size), BF16)] * 2,
        [*columns, teacher, *logits],
        (),
        after,
    )


def weight_blocks(hidden_t, slopes, first, count, start, size):
    return sum(
        jnp.dot(
            left[first : first + count, :],
            right[:, start : start + size],
            preferred_element_type=F32,
        )
        for left, right in zip(hidden_t, slopes)
    )


def weight_away_kernel(*refs, start):
    hidden_t, slopes, out = refs[:2], refs[2:4], refs[4]
    out[...] = weight_blocks(hidden_t, slopes, 0, out.shape[0], start, out.shape[1]).astype(BF16)


def weight_away(hidden_t, slopes, start, size, after=()):
    features = hidden_t[0].shape[0]
    return call(
        functools.partial(weight_away_kernel, start=start),
        "weight_away",
        [shape((features // 2, size), BF16)],
        [*hidden_t, *slopes],
        (),
        after,
    )[0]


def weight_home_kernel(*refs, start):
    hidden_t, slopes, received, outs = refs[:2], refs[2:4], refs[4], refs[5:]
    count, size = outs[0].shape
    for part, out in enumerate(outs):
        value = weight_blocks(hidden_t, slopes, (2 + part) * count, count, start, size)
        value += received[part * count : (part + 1) * count, :].astype(F32)
        out[...] = value.astype(BF16)


def weight_home(hidden_t, slopes, received, start, after=()):
    count, size = received.shape
    return call(
        functools.partial(weight_home_kernel, start=start),
        "weight_home",
        [shape((count // 2, size), BF16)] * 2,
        [*hidden_t, *slopes, received],
        (),
        after,
    )


def hidden_kernel(*refs, vocab_size, groups):
    *slopes, weight, away, home, rows = refs
    blocks = vocab_size
    height = rows.shape[0] // blocks
    begin = 0
    for at_part in range(0, len(slopes), groups):
        part = slopes[at_part : at_part + groups]
        columns = slice(begin, begin + part[0].shape[1])
        begin = columns.stop
        for i, block in enumerate(hidden_order(vocab_size)):
            to = slice(i * height, (i + 1) * height)
            if groups == 1:
                at = pl.multiple_of(block * height, height)
                rows[to, columns] = part[0][pl.ds(at, height), :]
                continue
            per = vocab_size // QUARTERS // 2
            at = pl.multiple_of((block // (2 * per) * per + block % per) * height, height)
            for group, slope in enumerate(part):

                @pl.when(block // per % 2 == group)
                def _():
                    rows[to, columns] = slope[pl.ds(at, height), :]

    value = rows[...]
    middle = away.shape[0]
    for start, size in tiles(0, weight.shape[0], 2 * LANES):
        at = slice(start, start + size)
        result = lax.dot_general(
            value, weight[at, :], (((1,), (1,)), ((), ())), preferred_element_type=F32
        )
        away[:, at] = result[:middle].astype(BF16)
        home[:, at] = result[middle:]


def hidden_blocks(slopes, weight, vocab_size, after=()):
    width = weight.shape[1]
    rows = sum(s.shape[0] for s in slopes[0])
    dims = (rows // 2, weight.shape[0])
    return call(
        functools.partial(hidden_kernel, vocab_size=vocab_size, groups=len(slopes[0])),
        "hidden_grad",
        [shape(dims, BF16), shape(dims, F32)],
        [*sum(slopes, []), weight],
        [pltpu.VMEM((rows, width), BF16)],
        after,
    )


def add_kernel(kept, received, *outs):
    count = outs[0].shape[0]
    for i, out in enumerate(outs):
        at = slice(i * count, (i + 1) * count)
        out[...] = (kept[at, :].astype(F32) + received[at, :].astype(F32)).astype(BF16)


def add(kept, received, parts, after=()):
    rows, width = kept.shape
    return call(
        add_kernel,
        "add",
        [shape((rows // parts, width), BF16)] * parts,
        [kept, received],
        (),
        after,
    )


def pack_kernel(kept, received, tokens, out):
    rows, width = kept.shape
    out[:, :width] = (kept[...].astype(F32) + received[...].astype(F32)).astype(BF16)
    rest, terms = tokens[...], []
    for _ in range(3):
        terms.append(rest.astype(BF16).astype(F32))
        rest = rest - terms[-1]
    rows_of = [fold(term[k : k + 1]) for term in terms for k in range(2)]
    room = rows * (out.shape[1] - width) // LANES
    values = pad_rows(jnp.concatenate(rows_of), room).astype(BF16)
    for i in range(room // rows):
        at = width + i * LANES
        out[:, at : at + LANES] = values[i * rows : (i + 1) * rows]


def pack(kept, received, tokens, after=()):
    rows, width = kept.shape
    need = 6 * tokens.shape[1] // LANES
    outs = [shape((rows, width + -(-need // rows) * LANES), BF16)]
    return call(pack_kernel, "pack", outs, [kept, received, tokens], (), after)


def tokens_kernel(strip, *values, width):
    folded = jnp.concatenate(
        [strip[:, at : at + LANES] for at in range(width, strip.shape[1], LANES)]
    ).astype(F32)
    for k, value in enumerate(values):
        size = value.shape[1]
        value[...] = sum(unfold(folded, k + 2 * term, size) for term in range(3))


def tokens_of(strip, rows, width, after):
    outs = [shape((1, rows), F32)] * 2
    kernel = functools.partial(tokens_kernel, width=width)
    return call(kernel, "tokens_of", outs, [strip], (), after)


def finish_kernel(*refs, start, so_far):
    kept, received, out, token, source, done = refs[so_far:]
    source[...] = (kept[...].astype(F32) + received[...].astype(F32)).astype(BF16)
    token[...] = jnp.zeros(token.shape, F32)
    run_copies(copy_pairs(source, out.at[:, start : start + source.shape[1]]), done)


def finish(parts, dims, start, so_far, after):
    return call(
        functools.partial(finish_kernel, start=start, so_far=len(so_far)),
        "finish",
        [pltpu.HBM(dims, BF16), shape((8, LANES), F32)],
        list(parts),
        [pltpu.VMEM(parts[0].shape, BF16), pltpu.SemaphoreType.DMA((8,))],
        after,
        so_far,
        bool(so_far),
    )


def local(hidden, out_weight, teacher_logits, token_ids, loss_mask):
    rows, features = hidden.shape
    width = out_weight.shape[1]
    vocab_size = lax.axis_size("vocab")
    group_axes, group_size = ("role", "dp"), lax.axis_size("role") * lax.axis_size("dp")
    assert lax.axis_size("role") == 2 and lax.axis_size("dp") == 4
    assert vocab_size & (vocab_size - 1) == 0 and vocab_size >= QUARTERS

    ids, mask = token_ids.reshape(1, rows), loss_mask.reshape(1, rows)
    pieces = []
    for k, piece in enumerate([(0, 0), (0, 1), (1, 0), (1, 1)]):
        pieces += pick_rows(hidden, [piece], (ids, mask) if k == 1 else (), after=pieces[-1:])
    direct = [xor_swap(piece, "role", 1) for piece in pieces]
    known = teacher_stats(teacher_logits, after=pieces[3:])
    direct[0] = pass_on(direct[0], [known])
    direct[1], side = unpack_rows(direct[1], rows)
    count = count_rows(side, mask)
    count = sum_rows(count, xor_swap(count, "dp", 1))
    direct[3] = pass_on(direct[3], [count])
    counts = [count, xor_swap(count, "dp", 2)]
    other = [xor_swap(piece, "vocab", 1) for piece in direct]

    logits, hidden_t, stats = [], [], []
    for group in range(2):
        pair = slice(2 * group, 2 * group + 2)
        done = group_logits(
            direct[pair],
            other[pair],
            out_weight,
            teacher_logits,
            side,
            known,
            stats[-1:],
            after=counts[1:] if group else direct[3:],
        )
        for values, value in zip((logits, stats), done):
            values.append(value)
        hidden_t.append(turn_rows(direct[pair], other[pair], after=stats[group:]))
    chunks = column_chunks(width, (7, 6, 6))
    split = chunks[1][0]
    slopes, tokens, columns = first_slopes(
        over_vocab(stats[1], vocab_size), side, counts, teacher_logits, logits, split, hidden_t[1:]
    )
    ranges = [(0, list(slopes))]
    last = slopes[1]

    def slope_step(last):
        slopes = more_slopes(columns, teacher_logits, logits, split, width - split, after=[last])
        ranges.append((split, list(slopes)))
        return slopes[1]

    by_group = vocab_size == QUARTERS
    home, hidden_in = [], []

    def hidden_step(last):
        k = len(home)
        if k == 0 or by_group:
            some = [s[k : k + 1] if by_group else s for _, s in ranges]
            last, kept = hidden_blocks(some, out_weight, vocab_size, after=[last])
            home.append(kept)
            hidden_in.append(xor_swap(last, "vocab", 1))
        return last

    arrived, near = [], []

    def chunk_of(k):
        start, size = chunks[k]
        begin, slopes = ranges[min(k, 1)]
        return slopes, start - begin, size

    def away_step(last):
        last = weight_away(hidden_t, *chunk_of(len(arrived)), after=[last])
        arrived.append(exchange(last, group_axes, group_size, lambda i: i ^ 1))
        return last

    def near_step(last):
        k = len(near)
        slopes, start, _ = chunk_of(k)
        leaving, last = weight_home(hidden_t, slopes, arrived[k], start, after=[last])
        near.append((last, exchange(leaving, group_axes, group_size, near_of)))
        return last

    far, grad_weight, returned, outs = [], [], [], []

    def far_step(last):
        kept, received = near[len(far)]
        leaving, last = add(kept, received, 2, after=[last])
        far.append((last, exchange(leaving, group_axes, group_size, far_of)))
        return last

    def weight_step(last):
        k = len(grad_weight)
        dims = (features // group_size, width)
        result, last = finish(far[k], dims, chunks[k][0], grad_weight[-1:], [last])
        grad_weight.append(result)
        return last

    halved = []

    def halve_step(last):
        if len(halved) < len(home):
            k = len(halved)
            leaving, last = add(home[k], hidden_in[k], 2, after=[last])
            halved.append((last, xor_swap(leaving, "vocab", 2)))
        return last

    def return_step(last):
        if len(returned) < len(home):
            kept, received = halved[len(returned)]
            bit = 4
            while bit < vocab_size:
                leaving, last = add(kept, received, 2, after=[last])
                kept, received = last, xor_swap(leaving, "vocab", bit)
                bit *= 2
            if returned:
                (last,) = add(kept, received, 1, after=[last])
            else:
                (last,) = pack(kept, received, tokens, after=[last])
            returned.append(xor_swap(last, "role", 1))
        return last

    def tokens_step(last):
        outs.extend(tokens_of(returned[0], rows, features, [last]))
        return outs[0]

    steps = {
        "s": slope_step,
        "a": away_step,
        "n": near_step,
        "h": hidden_step,
        "f": far_step,
        "v": halve_step,
        "r": return_step,
        "w": weight_step,
        "t": tokens_step,
    }
    for name in "asaanhnnhfvrfvwfwrtw":
        last = steps[name](last)

    grad_hidden = jnp.concatenate([r[:, :features] for r in returned])
    return outs[0].reshape(rows), outs[1].reshape(rows), grad_hidden, grad_weight[-1]


def solution(mesh):
    return jax.shard_map(
        local,
        mesh=mesh,
        in_specs=(
            P(("role", "dp"), None),
            P(None, "vocab"),
            P(("role", "dp"), "vocab"),
            P(("role", "dp")),
            P(("role", "dp")),
        ),
        out_specs=(
            P(("role", "dp")),
            P(("role", "dp")),
            P(("role", "dp", "vocab"), None),
            P(("role", "dp"), "vocab"),
        ),
        check_vma=False,
    )
```

```python
import functools

import jax
import jax.numpy as jnp
from jax import lax
from jax.experimental import pallas as pl
from jax.experimental.pallas import tpu as pltpu
from jax.sharding import PartitionSpec as P

F32 = jnp.float32
BF16 = jnp.bfloat16
VMEM_LIMIT = 18 * 1024 * 1024
LANES = 128
STEP = 16
LONG = 20_000_000_000
COST = 2_000_000_000
DIGIT = 128
BAND = 32
STATS = 8
QUARTERS = 4


def exchange(array, axes, size, partner):
    return lax.ppermute(array, axes, [(i, partner(i)) for i in range(size)])


def xor_swap(array, axis, mask):
    return exchange(array, axis, lax.axis_size(axis), lambda i: i ^ mask)


def shape(dims, dtype):
    return jax.ShapeDtypeStruct(dims, dtype)


def call(kernel, name, outs, arrays, scratch=(), after=(), far=(), aliases=False, flops=1024):
    skip = len(after)
    on_chip = pl.BlockSpec(memory_space=pltpu.VMEM)
    in_hbm = pl.BlockSpec(memory_space=pltpu.HBM)
    return pl.pallas_call(
        lambda *refs: kernel(*refs[skip:]),
        in_specs=[pl.BlockSpec(memory_space=pl.ANY)] * (skip + len(far))
        + [on_chip] * len(arrays),
        out_specs=[on_chip if isinstance(o, jax.ShapeDtypeStruct) else in_hbm for o in outs],
        out_shape=outs,
        scratch_shapes=list(scratch),
        input_output_aliases={skip: 0} if aliases else {},
        compiler_params=pltpu.CompilerParams(vmem_limit_bytes=VMEM_LIMIT),
        cost_estimate=pl.CostEstimate(flops=flops, bytes_accessed=1024, transcendentals=0),
        name=name,
    )(*after, *far, *arrays)


def column_chunks(width, shares):
    bounds = [width // LANES * sum(shares[:i]) // sum(shares) for i in range(len(shares) + 1)]
    return [(a * LANES, (b - a) * LANES) for a, b in zip(bounds, bounds[1:])]


def tiles(start, size, step):
    return [(at, min(step, start + size - at)) for at in range(start, start + size, step)]


def spread(row):
    return jnp.broadcast_to(row, (LANES, row.shape[1])).T


def lane_sum(ref):
    return jnp.sum(ref[...].T, axis=0, keepdims=True)


def fold(row):
    return jnp.concatenate([row[:, at : at + LANES] for at in range(0, row.shape[1], LANES)])


def unfold(values, k, count):
    each = count // LANES
    rows = [values[k * each + i : k * each + i + 1] for i in range(each)]
    return jnp.concatenate(rows, axis=1)


def pad_rows(values, rows):
    return jnp.concatenate([values, jnp.zeros((rows - values.shape[0], LANES), values.dtype)])


def row_steps(total, group):
    block = total // QUARTERS
    inside = block // 2

    def at(i):
        quarter, rest = i * STEP // inside, i * STEP % inside
        here = pl.multiple_of(i * STEP, STEP)
        there = pl.multiple_of(quarter * block + group * inside + rest, STEP)
        return pl.ds(here, STEP), pl.ds(there, STEP)

    return at


def copy_pairs(source, target, parts=4):
    rows = source.shape[0]
    size = max(STEP, -(-rows // parts) // STEP * STEP)
    return [
        (source.at[at : min(at + size, rows), :], target.at[at : min(at + size, rows), :])
        for at in range(0, rows, size)
    ]


def run_copies(pairs, done):
    copies = [pltpu.make_async_copy(*pair, done.at[i]) for i, pair in enumerate(pairs)]
    for copy in copies:
        copy.start()
    for copy in copies:
        copy.wait()


def near_of(index):
    return index ^ (2 if index & 1 else 4)


def far_of(index):
    return index ^ (4 if index & 1 else 2)


def weight_order():
    me = lax.axis_index("role") * 4 + lax.axis_index("dp")
    order = []
    for index in (me ^ 1, me):
        near = 4 - 2 * (index & 1)
        far = 6 - near
        order += [index ^ near ^ far, index ^ near, index ^ far, index]
    return order


def hidden_order(vocab_size):
    order = [lax.axis_index("vocab")]
    bit = vocab_size // 2
    while bit:
        order = [o ^ bit for o in order] + order
        bit //= 2
    return order


def pick_kernel(hidden, *refs, pieces, extra):
    sources, refs = refs[:extra], refs[extra:]
    outs, refs = refs[: len(pieces)], refs[len(pieces) :]
    landed, done = refs[:-1], refs[-1]
    odd = lax.axis_index("vocab") & 1
    block = hidden.shape[0] // QUARTERS
    size = block // 2
    pairs = list(zip(sources, landed))
    for (group, k), out in zip(pieces, outs):
        at = pl.multiple_of((2 * odd + k) * block + group * size, size)
        pairs += copy_pairs(hidden.at[pl.ds(at, size), :], out.at[:, : hidden.shape[1]])
    run_copies(pairs, done)
    if extra:
        ids, mask = (ref[...] for ref in landed)
        rest, terms = ids, []
        for _ in range(3):
            terms.append(rest & (DIGIT - 1))
            rest = rest >> (DIGIT.bit_length() - 1)
        values = jnp.concatenate([fold(v) for v in (*terms, mask)])
        outs[0][:, outs[0].shape[1] - LANES :] = pad_rows(values.astype(F32), size).astype(BF16)


def pick_rows(hidden, pieces, extra=(), after=()):
    rows, features = hidden.shape
    size = rows // QUARTERS // 2
    far = [pltpu.with_memory_space_constraint(a, pltpu.HBM) for a in (hidden, *extra)]
    more = [LANES if extra and i == 0 else 0 for i in range(len(pieces))]
    return call(
        functools.partial(pick_kernel, pieces=pieces, extra=len(extra)),
        "pick_rows",
        [shape((size, features + n), BF16) for n in more],
        [],
        [pltpu.VMEM((1, rows), jnp.int32)] * len(extra)
        + [pltpu.SemaphoreType.DMA((4 * len(pieces) + len(extra),))],
        after,
        far,
        flops=LONG,
    )


def unpack_kernel(packed, piece, side):
    features, count = piece.shape[1], side.shape[1]
    piece[...] = packed[:, :features]
    values = packed[:, features:].astype(F32)
    digits = [unfold(values, k, count) for k in range(4)]
    side[0:1, :] = digits[0] + DIGIT * (digits[1] + DIGIT * digits[2])
    side[1:2, :] = digits[3]


def unpack_rows(packed, rows):
    dims = (packed.shape[0], packed.shape[1] - LANES)
    return call(
        unpack_kernel,
        "unpack_rows",
        [shape(dims, BF16), shape((2, rows), F32)],
        [packed],
    )


def teacher_kernel(teacher, out, top, total):
    rows, width = teacher.shape

    @pl.loop(0, rows // STEP, unroll=2)
    def _(i):
        at = pl.ds(pl.multiple_of(i * STEP, STEP), STEP)
        best = teacher[at, 0:LANES]
        for start, size in tiles(LANES, width - LANES, LANES):
            best = jnp.maximum(best, teacher[at, start : start + size])
        top[at, :] = best.astype(F32)

    top_row = jnp.max(top[...].T, axis=0, keepdims=True)
    top[...] = spread(top_row)

    @pl.loop(0, rows // STEP, unroll=2)
    def _(i):
        at = pl.ds(pl.multiple_of(i * STEP, STEP), STEP)
        shift = top[at, :]
        acc = jnp.zeros((STEP, LANES), F32)
        for start, size in tiles(0, width, LANES):
            acc += jnp.exp(teacher[at, start : start + size].astype(F32) - shift)
        total[at, :] = acc

    out[...] = jnp.concatenate(
        [jnp.zeros((3, rows), F32), top_row, lane_sum(total), jnp.zeros((3, rows), F32)]
    )


def teacher_stats(teacher, after=()):
    rows, width = teacher.shape
    return call(
        teacher_kernel,
        "teacher_stats",
        [shape((STATS, rows), F32)],
        [teacher],
        [pltpu.VMEM((rows, LANES), F32)] * 2,
        after,
        flops=LONG,
    )[0]


def pass_on(array, after):
    outs = [shape(array.shape, array.dtype)]
    return call(lambda *refs: None, "pass_on", outs, [], (), after, [array], True)[0]


def count_kernel(side, mask, out):
    total = jnp.sum(side[1:2, :]) + jnp.sum(mask[...].astype(F32))
    out[...] = jnp.full(out.shape, total)


def sum_kernel(first, second, out):
    out[...] = first[...] + second[...]


def count_rows(side, mask):
    return call(count_kernel, "count_rows", [shape((8, LANES), F32)], [side, mask])[0]


def sum_rows(first, second):
    return call(sum_kernel, "sum_rows", [shape((8, LANES), F32)], [first, second])[0]


def gather_rows(direct, other, rows_in):
    odd = lax.axis_index("vocab") & 1
    half = rows_in.shape[0] // 2
    for first, refs in ((odd, direct), (1 - odd, other)):
        for i, ref in enumerate(refs):
            count = ref.shape[0]
            at = pl.multiple_of(first * half + i * count, count)
            rows_in[pl.ds(at, count), :] = ref[...]


def turn_rows(direct, other, after=()):
    count = len(direct)
    rows, features = 2 * count * direct[0].shape[0], direct[0].shape[1]

    def kernel(*refs):
        out, rows_in, turned = refs[2 * count :]
        gather_rows(refs[:count], refs[count : 2 * count], rows_in)
        turned[...] = rows_in[...].T
        height = features // 8
        for i, block in enumerate(weight_order()):
            at = pl.ds(pl.multiple_of(block * height, STEP), height)
            out[i * height : (i + 1) * height, :] = turned[at, :]

    return call(
        kernel,
        "turn_rows",
        [shape((features, rows), BF16)],
        [*direct, *other],
        [pltpu.VMEM((rows, features), BF16), pltpu.VMEM((features, rows), BF16)],
        after,
    )[0]


def logits_kernel(direct, other, weight, teacher, side, known, *refs):
    group = len(refs) - 8
    first, refs = refs[:group], refs[group:]
    logits, stats, rows_in, top, total, gap, picked, chosen = refs
    rows, width = logits.shape
    vocab = lax.axis_index("vocab")
    gather_rows(direct, other, rows_in)
    value = rows_in[...]

    ids = side[0:1, :] - (vocab * width).astype(F32)
    chosen[...] = spread(ids) - lax.broadcasted_iota(jnp.int32, chosen.shape, 1).astype(F32)
    for ref in (total, gap, picked):
        ref[...] = jnp.zeros(ref.shape, F32)
    inside = rows // QUARTERS
    for start, size in tiles(0, width, 2 * LANES):
        tile = jnp.dot(value, weight[:, start : start + size], preferred_element_type=F32)
        logits[:, start : start + size] = tile
        columns = range(start, start + size, LANES)
        for at in range(0, rows, BAND):
            here = slice(at, at + BAND)
            from_row = (at // inside * 2 + group) * inside + at % inside
            there = slice(from_row, from_row + BAND)
            students = [tile[here, c - start : c - start + LANES] for c in columns]
            best = functools.reduce(jnp.maximum, students)
            if start:
                last = top[here, :]
                best = jnp.maximum(best, last)
                scale = jnp.exp(last - best)
                sums = [total[there, :] * scale, gap[there, :] * scale]
                hit = picked[there, :]
            else:
                sums, hit = [0.0, 0.0], 0.0
            top[here, :] = best
            wanted = chosen[there, :]
            for c, student in zip(columns, students):
                target = teacher[there, c : c + LANES].astype(F32)
                share = jnp.exp(student - best)
                sums = [sums[0] + share, sums[1] + share * (student - target)]
                hit = hit + jnp.where(wanted == c, student, 0.0)
            total[there, :], gap[there, :], picked[there, :] = *sums, hit

    top_row = jnp.max(top[...].T, axis=0, keepdims=True)
    whole_top = spread(top_row)
    for at in range(0, rows, inside):
        here = slice(at, at + inside)
        from_row = (at // inside * 2 + group) * inside
        there = slice(from_row, from_row + inside)
        scale = jnp.exp(top[here, :] - whole_top[here, :])
        total[there, :] = total[there, :] * scale
        gap[there, :] = gap[there, :] * scale
        top[here, :] = whole_top[here, :]

    rows_known = {k: lane_sum(ref) for k, ref in ((1, total), (2, gap), (5, picked))}
    for q in range(QUARTERS):
        at = (2 * q + group) * inside
        total[at : at + inside, :] = top[q * inside : (q + 1) * inside, :]
    rows_known[0] = total[...].T[0:1, :]
    stats[...] = known[...]
    for k, row in rows_known.items():
        if first:
            lane = lax.broadcasted_iota(jnp.int32, row.shape, 1)
            row = jnp.where((lane & inside) != 0, row, first[0][k : k + 1, :])
        stats[k : k + 1, :] = row


def group_logits(direct, other, weight, teacher, side, known, first, after=()):
    rows, width = teacher.shape
    features = weight.shape[0]
    count = len(direct)

    def kernel(*refs):
        logits_kernel(refs[:count], refs[count : 2 * count], *refs[2 * count :])

    return call(
        kernel,
        "group_logits",
        [
            shape((rows // 2, width), F32),
            shape((STATS, rows), F32),
        ],
        [*direct, *other, weight, teacher, side, known, *first],
        [pltpu.VMEM((rows // 2, features), BF16)]
        + [pltpu.VMEM((rows // 2, LANES), F32)]
        + [pltpu.VMEM((rows, LANES), F32)] * 4,
        after,
        flops=LONG if first else COST,
    )


def join(parts):
    top = functools.reduce(jnp.maximum, [p[0] for p in parts])
    teacher_top = functools.reduce(jnp.maximum, [p[3] for p in parts])
    scales = [jnp.exp(p[0] - top) for p in parts]
    total = sum(s * p[1] for s, p in zip(scales, parts))
    gap = sum(s * p[2] for s, p in zip(scales, parts))
    teacher_total = sum(jnp.exp(p[3] - teacher_top) * p[4] for p in parts)
    picked = sum(p[5] for p in parts)
    return top, total, gap, teacher_top, teacher_total, picked


def over_vocab(stats, size):
    parts, done = [stats], 1
    while done < size:
        if done > 1:
            joined = join([[p[k] for k in range(6)] for p in parts])
            parts = [jnp.stack(list(joined) + [joined[0]] * (STATS - 6))]
        radix = min(4, size // done)
        parts += [xor_swap(parts[0], "vocab", k * done) for k in reversed(range(1, radix))]
        done *= radix
    return parts


def slope_kernel(*refs, parts):
    stats = refs[:parts]
    side, *counts, teacher, logits_0, logits_1 = refs[parts : parts + 6]
    slope_0, slope_1, tokens, lses, shifts, weights = refs[parts + 6 :]

    top, total, gap, teacher_top, teacher_total, picked = join(
        [[s[k : k + 1, :] for k in range(6)] for s in stats]
    )
    lse = top + jnp.log(total)
    diff = lse - (teacher_top + jnp.log(teacher_total))
    kl = gap / total - diff
    tokens[...] = jnp.concatenate([kl, picked - lse])
    mask_total = counts[0][0:1, 0:1] + counts[1][0:1, 0:1]
    lses[...] = spread(lse)
    shifts[...] = spread(diff + kl)
    weights[...] = spread(side[1:2, :] / jnp.maximum(mask_total, 1.0))
    for group, (logits, slope) in enumerate(((logits_0, slope_0), (logits_1, slope_1))):
        rows, width = logits.shape
        steps = row_steps(2 * rows, group)

        @pl.loop(0, rows // STEP, unroll=2)
        def _(i):
            here, there = steps(i)
            lse, shift, weight = lses[there, :], shifts[there, :], weights[there, :]
            for start, size in tiles(0, width, LANES):
                student = logits[here, start : start + size]
                target = teacher[there, start : start + size].astype(F32)
                value = weight * jnp.exp(student - lse) * (student - target - shift)
                slope[here, start : start + size] = value.astype(BF16)


def slopes_of(stats, side, counts, teacher, logits, after=()):
    rows, width = teacher.shape
    return call(
        functools.partial(slope_kernel, parts=len(stats)),
        "slopes",
        [shape((rows // 2, width), BF16)] * 2 + [shape((2, rows), F32)],
        [*stats, side, *counts, teacher, *logits],
        [pltpu.VMEM((rows, LANES), F32)] * 3,
        after,
    )


def weight_blocks(hidden_t, slopes, first, count, start, size):
    return sum(
        jnp.dot(
            left[first : first + count, :],
            right[:, start : start + size],
            preferred_element_type=F32,
        )
        for left, right in zip(hidden_t, slopes)
    )


def weight_away_kernel(*refs, start):
    hidden_t, slopes, out = refs[:2], refs[2:4], refs[4]
    out[...] = weight_blocks(hidden_t, slopes, 0, out.shape[0], start, out.shape[1]).astype(BF16)


def weight_away(hidden_t, slopes, start, size, after=()):
    features = hidden_t[0].shape[0]
    return call(
        functools.partial(weight_away_kernel, start=start),
        "weight_away",
        [shape((features // 2, size), BF16)],
        [*hidden_t, *slopes],
        (),
        after,
    )[0]


def weight_home_kernel(*refs, start):
    hidden_t, slopes, received, outs = refs[:2], refs[2:4], refs[4], refs[5:]
    count, size = outs[0].shape
    for part, out in enumerate(outs):
        value = weight_blocks(hidden_t, slopes, (2 + part) * count, count, start, size)
        value += received[part * count : (part + 1) * count, :].astype(F32)
        out[...] = value.astype(BF16)


def weight_home(hidden_t, slopes, received, start, after=()):
    count, size = received.shape
    return call(
        functools.partial(weight_home_kernel, start=start),
        "weight_home",
        [shape((count // 2, size), BF16)] * 2,
        [*hidden_t, *slopes, received],
        (),
        after,
    )


def hidden_kernel(*refs, vocab_size):
    *slopes, weight, away, home, rows = refs
    blocks = vocab_size
    height = rows.shape[0] // blocks
    for i, block in enumerate(hidden_order(vocab_size)):
        to = slice(i * height, (i + 1) * height)
        if len(slopes) == 1:
            rows[to, :] = slopes[0][pl.ds(pl.multiple_of(block * height, height), height), :]
        else:
            per = vocab_size // QUARTERS // 2
            at = (block // (2 * per) * per + block % per) * height
            for group, slope in enumerate(slopes):

                @pl.when(block // per % 2 == group)
                def _():
                    rows[to, :] = slope[pl.ds(pl.multiple_of(at, height), height), :]

    value = rows[...]
    middle = away.shape[0]
    for start, size in tiles(0, weight.shape[0], 2 * LANES):
        at = slice(start, start + size)
        result = lax.dot_general(
            value, weight[at, :], (((1,), (1,)), ((), ())), preferred_element_type=F32
        )
        away[:, at] = result[:middle].astype(BF16)
        home[:, at] = result[middle:]


def hidden_blocks(slopes, weight, vocab_size, after=()):
    width = weight.shape[1]
    rows = sum(s.shape[0] for s in slopes)
    dims = (rows // 2, weight.shape[0])
    return call(
        functools.partial(hidden_kernel, vocab_size=vocab_size),
        "hidden_grad",
        [shape(dims, BF16), shape(dims, F32)],
        [*slopes, weight],
        [pltpu.VMEM((rows, width), BF16)],
        after,
    )


def add_kernel(kept, received, *outs):
    count = outs[0].shape[0]
    for i, out in enumerate(outs):
        at = slice(i * count, (i + 1) * count)
        out[...] = (kept[at, :].astype(F32) + received[at, :].astype(F32)).astype(BF16)


def add(kept, received, parts, after=()):
    rows, width = kept.shape
    return call(
        add_kernel,
        "add",
        [shape((rows // parts, width), BF16)] * parts,
        [kept, received],
        (),
        after,
    )


def pack_kernel(kept, received, tokens, out):
    rows, width = kept.shape
    out[:, :width] = (kept[...].astype(F32) + received[...].astype(F32)).astype(BF16)
    rest, terms = tokens[...], []
    for _ in range(3):
        terms.append(rest.astype(BF16).astype(F32))
        rest = rest - terms[-1]
    rows_of = [fold(term[k : k + 1]) for term in terms for k in range(2)]
    room = rows * (out.shape[1] - width) // LANES
    values = pad_rows(jnp.concatenate(rows_of), room).astype(BF16)
    for i in range(room // rows):
        at = width + i * LANES
        out[:, at : at + LANES] = values[i * rows : (i + 1) * rows]


def pack(kept, received, tokens, after=()):
    rows, width = kept.shape
    need = 6 * tokens.shape[1] // LANES
    outs = [shape((rows, width + -(-need // rows) * LANES), BF16)]
    return call(pack_kernel, "pack", outs, [kept, received, tokens], (), after)


def tokens_kernel(strip, *values, width):
    folded = jnp.concatenate(
        [strip[:, at : at + LANES] for at in range(width, strip.shape[1], LANES)]
    ).astype(F32)
    for k, value in enumerate(values):
        size = value.shape[1]
        value[...] = sum(unfold(folded, k + 2 * term, size) for term in range(3))


def tokens_of(strip, rows, width, after):
    outs = [shape((1, rows), F32)] * 2
    kernel = functools.partial(tokens_kernel, width=width)
    return call(kernel, "tokens_of", outs, [strip], (), after)


def finish_kernel(*refs, start, so_far):
    kept, received, out, token, source, done = refs[so_far:]
    source[...] = (kept[...].astype(F32) + received[...].astype(F32)).astype(BF16)
    token[...] = jnp.zeros(token.shape, F32)
    run_copies(copy_pairs(source, out.at[:, start : start + source.shape[1]]), done)


def finish(parts, dims, start, so_far, after):
    return call(
        functools.partial(finish_kernel, start=start, so_far=len(so_far)),
        "finish",
        [pltpu.HBM(dims, BF16), shape((8, LANES), F32)],
        list(parts),
        [pltpu.VMEM(parts[0].shape, BF16), pltpu.SemaphoreType.DMA((8,))],
        after,
        so_far,
        bool(so_far),
    )


def local(hidden, out_weight, teacher_logits, token_ids, loss_mask):
    rows, features = hidden.shape
    width = out_weight.shape[1]
    vocab_size = lax.axis_size("vocab")
    group_axes, group_size = ("role", "dp"), lax.axis_size("role") * lax.axis_size("dp")
    assert lax.axis_size("role") == 2 and lax.axis_size("dp") == 4
    assert vocab_size & (vocab_size - 1) == 0 and vocab_size >= QUARTERS

    ids, mask = token_ids.reshape(1, rows), loss_mask.reshape(1, rows)
    pieces = list(pick_rows(hidden, [(0, 0)]))
    pieces += pick_rows(hidden, [(0, 1), (1, 0), (1, 1)], (ids, mask), after=pieces)
    direct = [xor_swap(piece, "role", 1) for piece in pieces]
    known = teacher_stats(teacher_logits, after=pieces[1:2])
    direct[0] = pass_on(direct[0], [known])
    direct[1], side = unpack_rows(direct[1], rows)
    count = count_rows(side, mask)
    count = sum_rows(count, xor_swap(count, "dp", 1))
    direct[2] = pass_on(direct[2], [count])
    counts = [count, xor_swap(count, "dp", 2)]
    other = [xor_swap(piece, "vocab", 1) for piece in direct]

    logits, hidden_t, stats = [], [], []
    for group in range(2):
        pair = slice(2 * group, 2 * group + 2)
        done = group_logits(
            direct[pair],
            other[pair],
            out_weight,
            teacher_logits,
            side,
            known,
            stats[-1:],
            after=counts[1:] if group else direct[3:],
        )
        for values, value in zip((logits, stats), done):
            values.append(value)
        hidden_t.append(turn_rows(direct[pair], other[pair], after=stats[group:]))
    *slopes, tokens = slopes_of(
        over_vocab(stats[1], vocab_size), side, counts, teacher_logits, logits, hidden_t[1:]
    )

    parts = [[s] for s in slopes] if vocab_size == QUARTERS else [slopes]
    home, hidden_in = [], []

    def hidden_step(last):
        if len(home) < len(parts):
            some = parts[len(home)]
            last, kept = hidden_blocks(some, out_weight, vocab_size, after=[last])
            home.append(kept)
            hidden_in.append(xor_swap(last, "vocab", 1))
        return last

    chunks = column_chunks(width, (7, 6, 6))
    arrived, near = [], []

    def away_step(last):
        last = weight_away(hidden_t, slopes, *chunks[len(arrived)], after=[last])
        arrived.append(exchange(last, group_axes, group_size, lambda i: i ^ 1))
        return last

    def near_step(last):
        k = len(near)
        leaving, last = weight_home(hidden_t, slopes, arrived[k], chunks[k][0], after=[last])
        near.append((last, exchange(leaving, group_axes, group_size, near_of)))
        return last

    far, grad_weight, returned, outs = [], [], [], []

    def far_step(last):
        kept, received = near[len(far)]
        leaving, last = add(kept, received, 2, after=[last])
        far.append((last, exchange(leaving, group_axes, group_size, far_of)))
        return last

    def weight_step(last):
        k = len(grad_weight)
        dims = (features // group_size, width)
        result, last = finish(far[k], dims, chunks[k][0], grad_weight[-1:], [last])
        grad_weight.append(result)
        return last

    halved = []

    def halve_step(last):
        if len(halved) < len(home):
            k = len(halved)
            leaving, last = add(home[k], hidden_in[k], 2, after=[last])
            halved.append((last, xor_swap(leaving, "vocab", 2)))
        return last

    def return_step(last):
        if len(returned) < len(home):
            kept, received = halved[len(returned)]
            bit = 4
            while bit < vocab_size:
                leaving, last = add(kept, received, 2, after=[last])
                kept, received = last, xor_swap(leaving, "vocab", bit)
                bit *= 2
            if returned:
                (last,) = add(kept, received, 1, after=[last])
            else:
                (last,) = pack(kept, received, tokens, after=[last])
            returned.append(xor_swap(last, "role", 1))
        return last

    def tokens_step(last):
        outs.extend(tokens_of(returned[0], rows, features, [last]))
        return outs[0]

    last = slopes[1]
    steps = {
        "a": away_step,
        "n": near_step,
        "h": hidden_step,
        "f": far_step,
        "v": halve_step,
        "r": return_step,
        "w": weight_step,
        "t": tokens_step,
    }
    for name in "aaanhnnhfvrfvfwwrtw":
        step = steps[name]
        last = step(last)

    grad_hidden = jnp.concatenate([r[:, :features] for r in returned])
    return outs[0].reshape(rows), outs[1].reshape(rows), grad_hidden, grad_weight[-1]


def solution(mesh):
    return jax.shard_map(
        local,
        mesh=mesh,
        in_specs=(
            P(("role", "dp"), None),
            P(None, "vocab"),
            P(("role", "dp"), "vocab"),
            P(("role", "dp")),
            P(("role", "dp")),
        ),
        out_specs=(
            P(("role", "dp")),
            P(("role", "dp")),
            P(("role", "dp", "vocab"), None),
            P(("role", "dp"), "vocab"),
        ),
        check_vma=False,
    )
```

```python
import functools

import jax
import jax.numpy as jnp
from jax import lax
from jax.experimental import pallas as pl
from jax.experimental.pallas import tpu as pltpu
from jax.sharding import PartitionSpec as P

F32 = jnp.float32
BF16 = jnp.bfloat16
VMEM_LIMIT = 18 * 1024 * 1024
LANES = 128
STEP = 16
LONG = 20_000_000_000
COST = 2_000_000_000
DIGIT = 128
BAND = 32
STATS = 8
QUARTERS = 4


def exchange(array, axes, size, partner):
    return lax.ppermute(array, axes, [(i, partner(i)) for i in range(size)])


def xor_swap(array, axis, mask):
    return exchange(array, axis, lax.axis_size(axis), lambda i: i ^ mask)


def shape(dims, dtype):
    return jax.ShapeDtypeStruct(dims, dtype)


def call(kernel, name, outs, arrays, scratch=(), after=(), far=(), aliases=False, flops=1024):
    skip = len(after)
    on_chip = pl.BlockSpec(memory_space=pltpu.VMEM)
    in_hbm = pl.BlockSpec(memory_space=pltpu.HBM)
    return pl.pallas_call(
        lambda *refs: kernel(*refs[skip:]),
        in_specs=[pl.BlockSpec(memory_space=pl.ANY)] * (skip + len(far))
        + [on_chip] * len(arrays),
        out_specs=[on_chip if isinstance(o, jax.ShapeDtypeStruct) else in_hbm for o in outs],
        out_shape=outs,
        scratch_shapes=list(scratch),
        input_output_aliases={skip: 0} if aliases else {},
        compiler_params=pltpu.CompilerParams(vmem_limit_bytes=VMEM_LIMIT),
        cost_estimate=pl.CostEstimate(flops=flops, bytes_accessed=1024, transcendentals=0),
        name=name,
    )(*after, *far, *arrays)


def column_chunks(width, shares):
    bounds = [width // LANES * sum(shares[:i]) // sum(shares) for i in range(len(shares) + 1)]
    return [(a * LANES, (b - a) * LANES) for a, b in zip(bounds, bounds[1:])]


def tiles(start, size, step):
    return [(at, min(step, start + size - at)) for at in range(start, start + size, step)]


def spread(row):
    return jnp.broadcast_to(row, (LANES, row.shape[1])).T


def lane_sum(ref):
    return jnp.sum(ref[...].T, axis=0, keepdims=True)


def fold(row):
    return jnp.concatenate([row[:, at : at + LANES] for at in range(0, row.shape[1], LANES)])


def unfold(values, k, count):
    each = count // LANES
    rows = [values[k * each + i : k * each + i + 1] for i in range(each)]
    return jnp.concatenate(rows, axis=1)


def pad_rows(values, rows):
    return jnp.concatenate([values, jnp.zeros((rows - values.shape[0], LANES), values.dtype)])


def row_steps(total, group):
    block = total // QUARTERS
    inside = block // 2

    def at(i):
        quarter, rest = i * STEP // inside, i * STEP % inside
        here = pl.multiple_of(i * STEP, STEP)
        there = pl.multiple_of(quarter * block + group * inside + rest, STEP)
        return pl.ds(here, STEP), pl.ds(there, STEP)

    return at


def copy_pairs(source, target, parts=4):
    rows = source.shape[0]
    size = max(STEP, -(-rows // parts) // STEP * STEP)
    return [
        (source.at[at : min(at + size, rows), :], target.at[at : min(at + size, rows), :])
        for at in range(0, rows, size)
    ]


def run_copies(pairs, done):
    copies = [pltpu.make_async_copy(*pair, done.at[i]) for i, pair in enumerate(pairs)]
    for copy in copies:
        copy.start()
    for copy in copies:
        copy.wait()


def near_of(index):
    return index ^ (2 if index & 1 else 4)


def far_of(index):
    return index ^ (4 if index & 1 else 2)


def weight_order():
    me = lax.axis_index("role") * 4 + lax.axis_index("dp")
    order = []
    for index in (me ^ 1, me):
        near = 4 - 2 * (index & 1)
        far = 6 - near
        order += [index ^ near ^ far, index ^ near, index ^ far, index]
    return order


def hidden_order(vocab_size):
    order = [lax.axis_index("vocab")]
    bit = vocab_size // 2
    while bit:
        order = [o ^ bit for o in order] + order
        bit //= 2
    return order


def pick_kernel(hidden, *refs, pieces, extra):
    sources, refs = refs[:extra], refs[extra:]
    outs, refs = refs[: len(pieces)], refs[len(pieces) :]
    landed, done = refs[:-1], refs[-1]
    odd = lax.axis_index("vocab") & 1
    block = hidden.shape[0] // QUARTERS
    size = block // 2
    pairs = list(zip(sources, landed))
    for (group, k), out in zip(pieces, outs):
        at = pl.multiple_of((2 * odd + k) * block + group * size, size)
        pairs += copy_pairs(hidden.at[pl.ds(at, size), :], out.at[:, : hidden.shape[1]])
    run_copies(pairs, done)
    if extra:
        ids, mask = (ref[...] for ref in landed)
        rest, terms = ids, []
        for _ in range(3):
            terms.append(rest & (DIGIT - 1))
            rest = rest >> (DIGIT.bit_length() - 1)
        values = jnp.concatenate([fold(v) for v in (*terms, mask)])
        outs[0][:, outs[0].shape[1] - LANES :] = pad_rows(values.astype(F32), size).astype(BF16)


def pick_rows(hidden, pieces, extra=(), after=()):
    rows, features = hidden.shape
    size = rows // QUARTERS // 2
    far = [pltpu.with_memory_space_constraint(a, pltpu.HBM) for a in (hidden, *extra)]
    more = [LANES if extra and i == 0 else 0 for i in range(len(pieces))]
    return call(
        functools.partial(pick_kernel, pieces=pieces, extra=len(extra)),
        "pick_rows",
        [shape((size, features + n), BF16) for n in more],
        [],
        [pltpu.VMEM((1, rows), jnp.int32)] * len(extra)
        + [pltpu.SemaphoreType.DMA((4 * len(pieces) + len(extra),))],
        after,
        far,
        flops=LONG,
    )


def unpack_kernel(packed, piece, side):
    features, count = piece.shape[1], side.shape[1]
    piece[...] = packed[:, :features]
    values = packed[:, features:].astype(F32)
    digits = [unfold(values, k, count) for k in range(4)]
    side[0:1, :] = digits[0] + DIGIT * (digits[1] + DIGIT * digits[2])
    side[1:2, :] = digits[3]


def unpack_rows(packed, rows):
    dims = (packed.shape[0], packed.shape[1] - LANES)
    return call(
        unpack_kernel,
        "unpack_rows",
        [shape(dims, BF16), shape((2, rows), F32)],
        [packed],
    )


def teacher_kernel(teacher, out, top, total):
    rows, width = teacher.shape

    @pl.loop(0, rows // STEP, unroll=2)
    def _(i):
        at = pl.ds(pl.multiple_of(i * STEP, STEP), STEP)
        best = teacher[at, 0:LANES]
        for start, size in tiles(LANES, width - LANES, LANES):
            best = jnp.maximum(best, teacher[at, start : start + size])
        top[at, :] = best.astype(F32)

    top_row = jnp.max(top[...].T, axis=0, keepdims=True)
    top[...] = spread(top_row)

    @pl.loop(0, rows // STEP, unroll=2)
    def _(i):
        at = pl.ds(pl.multiple_of(i * STEP, STEP), STEP)
        shift = top[at, :]
        acc = jnp.zeros((STEP, LANES), F32)
        for start, size in tiles(0, width, LANES):
            acc += jnp.exp(teacher[at, start : start + size].astype(F32) - shift)
        total[at, :] = acc

    out[...] = jnp.concatenate(
        [jnp.zeros((3, rows), F32), top_row, lane_sum(total), jnp.zeros((3, rows), F32)]
    )


def teacher_stats(teacher, after=()):
    rows, width = teacher.shape
    return call(
        teacher_kernel,
        "teacher_stats",
        [shape((STATS, rows), F32)],
        [teacher],
        [pltpu.VMEM((rows, LANES), F32)] * 2,
        after,
        flops=LONG,
    )[0]


def pass_on(array, after):
    outs = [shape(array.shape, array.dtype)]
    return call(lambda *refs: None, "pass_on", outs, [], (), after, [array], True)[0]


def count_kernel(side, mask, out):
    total = jnp.sum(side[1:2, :]) + jnp.sum(mask[...].astype(F32))
    out[...] = jnp.full(out.shape, total)


def sum_kernel(first, second, out):
    out[...] = first[...] + second[...]


def count_rows(side, mask):
    return call(count_kernel, "count_rows", [shape((8, LANES), F32)], [side, mask])[0]


def sum_rows(first, second):
    return call(sum_kernel, "sum_rows", [shape((8, LANES), F32)], [first, second])[0]


def gather_rows(direct, other, rows_in):
    odd = lax.axis_index("vocab") & 1
    half = rows_in.shape[0] // 2
    for first, refs in ((odd, direct), (1 - odd, other)):
        for i, ref in enumerate(refs):
            count = ref.shape[0]
            at = pl.multiple_of(first * half + i * count, count)
            rows_in[pl.ds(at, count), :] = ref[...]


def turn_rows(direct, other, after=()):
    count = len(direct)
    rows, features = 2 * count * direct[0].shape[0], direct[0].shape[1]

    def kernel(*refs):
        out, rows_in, turned = refs[2 * count :]
        gather_rows(refs[:count], refs[count : 2 * count], rows_in)
        turned[...] = rows_in[...].T
        height = features // 8
        for i, block in enumerate(weight_order()):
            at = pl.ds(pl.multiple_of(block * height, STEP), height)
            out[i * height : (i + 1) * height, :] = turned[at, :]

    return call(
        kernel,
        "turn_rows",
        [shape((features, rows), BF16)],
        [*direct, *other],
        [pltpu.VMEM((rows, features), BF16), pltpu.VMEM((features, rows), BF16)],
        after,
    )[0]


def logits_kernel(direct, other, weight, teacher, side, known, *refs):
    group = len(refs) - 8
    first, refs = refs[:group], refs[group:]
    logits, stats, rows_in, top, total, gap, picked, chosen = refs
    rows, width = logits.shape
    vocab = lax.axis_index("vocab")
    gather_rows(direct, other, rows_in)
    value = rows_in[...]

    ids = side[0:1, :] - (vocab * width).astype(F32)
    chosen[...] = spread(ids) - lax.broadcasted_iota(jnp.int32, chosen.shape, 1).astype(F32)
    for ref in (total, gap, picked):
        ref[...] = jnp.zeros(ref.shape, F32)
    inside = rows // QUARTERS
    for start, size in tiles(0, width, 2 * LANES):
        tile = jnp.dot(value, weight[:, start : start + size], preferred_element_type=F32)
        logits[:, start : start + size] = tile
        columns = range(start, start + size, LANES)
        for at in range(0, rows, BAND):
            here = slice(at, at + BAND)
            from_row = (at // inside * 2 + group) * inside + at % inside
            there = slice(from_row, from_row + BAND)
            students = [tile[here, c - start : c - start + LANES] for c in columns]
            best = functools.reduce(jnp.maximum, students)
            if start:
                last = top[here, :]
                best = jnp.maximum(best, last)
                scale = jnp.exp(last - best)
                sums = [total[there, :] * scale, gap[there, :] * scale]
                hit = picked[there, :]
            else:
                sums, hit = [0.0, 0.0], 0.0
            top[here, :] = best
            wanted = chosen[there, :]
            for c, student in zip(columns, students):
                target = teacher[there, c : c + LANES].astype(F32)
                share = jnp.exp(student - best)
                sums = [sums[0] + share, sums[1] + share * (student - target)]
                hit = hit + jnp.where(wanted == c, student, 0.0)
            total[there, :], gap[there, :], picked[there, :] = *sums, hit

    top_row = jnp.max(top[...].T, axis=0, keepdims=True)
    whole_top = spread(top_row)
    for at in range(0, rows, inside):
        here = slice(at, at + inside)
        from_row = (at // inside * 2 + group) * inside
        there = slice(from_row, from_row + inside)
        scale = jnp.exp(top[here, :] - whole_top[here, :])
        total[there, :] = total[there, :] * scale
        gap[there, :] = gap[there, :] * scale
        top[here, :] = whole_top[here, :]

    rows_known = {k: lane_sum(ref) for k, ref in ((1, total), (2, gap), (5, picked))}
    for q in range(QUARTERS):
        at = (2 * q + group) * inside
        total[at : at + inside, :] = top[q * inside : (q + 1) * inside, :]
    rows_known[0] = total[...].T[0:1, :]
    stats[...] = known[...]
    for k, row in rows_known.items():
        if first:
            lane = lax.broadcasted_iota(jnp.int32, row.shape, 1)
            row = jnp.where((lane & inside) != 0, row, first[0][k : k + 1, :])
        stats[k : k + 1, :] = row


def group_logits(direct, other, weight, teacher, side, known, first, after=()):
    rows, width = teacher.shape
    features = weight.shape[0]
    count = len(direct)

    def kernel(*refs):
        logits_kernel(refs[:count], refs[count : 2 * count], *refs[2 * count :])

    return call(
        kernel,
        "group_logits",
        [
            shape((rows // 2, width), F32),
            shape((STATS, rows), F32),
        ],
        [*direct, *other, weight, teacher, side, known, *first],
        [pltpu.VMEM((rows // 2, features), BF16)]
        + [pltpu.VMEM((rows // 2, LANES), F32)]
        + [pltpu.VMEM((rows, LANES), F32)] * 4,
        after,
        flops=LONG if first else COST,
    )


def join(parts):
    top = functools.reduce(jnp.maximum, [p[0] for p in parts])
    teacher_top = functools.reduce(jnp.maximum, [p[3] for p in parts])
    scales = [jnp.exp(p[0] - top) for p in parts]
    total = sum(s * p[1] for s, p in zip(scales, parts))
    gap = sum(s * p[2] for s, p in zip(scales, parts))
    teacher_total = sum(jnp.exp(p[3] - teacher_top) * p[4] for p in parts)
    picked = sum(p[5] for p in parts)
    return top, total, gap, teacher_top, teacher_total, picked


def over_vocab(stats, size):
    parts, done = [stats], 1
    while done < size:
        if done > 1:
            joined = join([[p[k] for k in range(6)] for p in parts])
            parts = [jnp.stack(list(joined) + [joined[0]] * (STATS - 6))]
        radix = min(4, size // done)
        parts += [xor_swap(parts[0], "vocab", k * done) for k in range(1, radix)]
        done *= radix
    return parts


def row_kernel(stats, side, counts, tokens, lses, shifts, weights):
    top, total, gap, teacher_top, teacher_total, picked = join(
        [[s[k : k + 1, :] for k in range(6)] for s in stats]
    )
    lse = top + jnp.log(total)
    diff = lse - (teacher_top + jnp.log(teacher_total))
    kl = gap / total - diff
    tokens[...] = jnp.concatenate([kl, picked - lse])
    mask_total = counts[0][0:1, 0:1] + counts[1][0:1, 0:1]
    lses[...] = spread(lse)
    shifts[...] = spread(diff + kl)
    weights[...] = spread(side[1:2, :] / jnp.maximum(mask_total, 1.0))


def slope_kernel(lses, shifts, weights, teacher, *refs, start):
    for group, (logits, slope) in enumerate(zip(refs[:2], refs[2:])):
        rows, width = slope.shape
        steps = row_steps(2 * rows, group)

        @pl.loop(0, rows // STEP, unroll=2)
        def _(i):
            here, there = steps(i)
            lse, shift, weight = lses[there, :], shifts[there, :], weights[there, :]
            for at, size in tiles(0, width, LANES):
                student = logits[here, start + at : start + at + size]
                target = teacher[there, start + at : start + at + size].astype(F32)
                value = weight * jnp.exp(student - lse) * (student - target - shift)
                slope[here, at : at + size] = value.astype(BF16)


def first_slopes(stats, side, counts, teacher, logits, size, after=()):
    rows = teacher.shape[0]
    parts = len(stats)

    def kernel(*refs):
        before, (slope_0, slope_1, *after) = refs[: parts + 6], refs[parts + 6 :]
        side, first, second, teacher, *logits = before[parts:]
        row_kernel(before[:parts], side, (first, second), *after)
        slope_kernel(*after[1:], teacher, *logits, slope_0, slope_1, start=0)

    *slopes, tokens, lses, shifts, weights = call(
        kernel,
        "slopes",
        [shape((rows // 2, size), BF16)] * 2
        + [shape((2, rows), F32)]
        + [shape((rows, LANES), F32)] * 3,
        [*stats, side, *counts, teacher, *logits],
        (),
        after,
    )
    return slopes, tokens, (lses, shifts, weights)


def more_slopes(columns, teacher, logits, start, size, after=()):
    rows = teacher.shape[0]
    return call(
        functools.partial(slope_kernel, start=start),
        "slopes",
        [shape((rows // 2, size), BF16)] * 2,
        [*columns, teacher, *logits],
        (),
        after,
    )


def weight_blocks(hidden_t, slopes, first, count, start, size):
    return sum(
        jnp.dot(
            left[first : first + count, :],
            right[:, start : start + size],
            preferred_element_type=F32,
        )
        for left, right in zip(hidden_t, slopes)
    )


def weight_away_kernel(*refs, start):
    hidden_t, slopes, out = refs[:2], refs[2:4], refs[4]
    out[...] = weight_blocks(hidden_t, slopes, 0, out.shape[0], start, out.shape[1]).astype(BF16)


def weight_away(hidden_t, slopes, start, size, after=()):
    features = hidden_t[0].shape[0]
    return call(
        functools.partial(weight_away_kernel, start=start),
        "weight_away",
        [shape((features // 2, size), BF16)],
        [*hidden_t, *slopes],
        (),
        after,
    )[0]


def weight_home_kernel(*refs, start):
    hidden_t, slopes, received, outs = refs[:2], refs[2:4], refs[4], refs[5:]
    count, size = outs[0].shape
    for part, out in enumerate(outs):
        value = weight_blocks(hidden_t, slopes, (2 + part) * count, count, start, size)
        value += received[part * count : (part + 1) * count, :].astype(F32)
        out[...] = value.astype(BF16)


def weight_home(hidden_t, slopes, received, start, after=()):
    count, size = received.shape
    return call(
        functools.partial(weight_home_kernel, start=start),
        "weight_home",
        [shape((count // 2, size), BF16)] * 2,
        [*hidden_t, *slopes, received],
        (),
        after,
    )


def hidden_kernel(*refs, vocab_size, groups):
    *slopes, weight, away, home, rows = refs
    blocks = vocab_size
    height = rows.shape[0] // blocks
    begin = 0
    for at_part in range(0, len(slopes), groups):
        part = slopes[at_part : at_part + groups]
        columns = slice(begin, begin + part[0].shape[1])
        begin = columns.stop
        for i, block in enumerate(hidden_order(vocab_size)):
            to = slice(i * height, (i + 1) * height)
            if groups == 1:
                at = pl.multiple_of(block * height, height)
                rows[to, columns] = part[0][pl.ds(at, height), :]
                continue
            per = vocab_size // QUARTERS // 2
            at = pl.multiple_of((block // (2 * per) * per + block % per) * height, height)
            for group, slope in enumerate(part):

                @pl.when(block // per % 2 == group)
                def _():
                    rows[to, columns] = slope[pl.ds(at, height), :]

    value = rows[...]
    middle = away.shape[0]
    for start, size in tiles(0, weight.shape[0], 2 * LANES):
        at = slice(start, start + size)
        result = lax.dot_general(
            value, weight[at, :], (((1,), (1,)), ((), ())), preferred_element_type=F32
        )
        away[:, at] = result[:middle].astype(BF16)
        home[:, at] = result[middle:]


def hidden_blocks(slopes, weight, vocab_size, after=()):
    width = weight.shape[1]
    rows = sum(s.shape[0] for s in slopes[0])
    dims = (rows // 2, weight.shape[0])
    return call(
        functools.partial(hidden_kernel, vocab_size=vocab_size, groups=len(slopes[0])),
        "hidden_grad",
        [shape(dims, BF16), shape(dims, F32)],
        [*sum(slopes, []), weight],
        [pltpu.VMEM((rows, width), BF16)],
        after,
    )


def add_kernel(kept, received, *outs):
    count = outs[0].shape[0]
    for i, out in enumerate(outs):
        at = slice(i * count, (i + 1) * count)
        out[...] = (kept[at, :].astype(F32) + received[at, :].astype(F32)).astype(BF16)


def add(kept, received, parts, after=()):
    rows, width = kept.shape
    return call(
        add_kernel,
        "add",
        [shape((rows // parts, width), BF16)] * parts,
        [kept, received],
        (),
        after,
    )


def pack_kernel(kept, received, tokens, out):
    rows, width = kept.shape
    out[:, :width] = (kept[...].astype(F32) + received[...].astype(F32)).astype(BF16)
    rest, terms = tokens[...], []
    for _ in range(3):
        terms.append(rest.astype(BF16).astype(F32))
        rest = rest - terms[-1]
    rows_of = [fold(term[k : k + 1]) for term in terms for k in range(2)]
    room = rows * (out.shape[1] - width) // LANES
    values = pad_rows(jnp.concatenate(rows_of), room).astype(BF16)
    for i in range(room // rows):
        at = width + i * LANES
        out[:, at : at + LANES] = values[i * rows : (i + 1) * rows]


def pack(kept, received, tokens, after=()):
    rows, width = kept.shape
    need = 6 * tokens.shape[1] // LANES
    outs = [shape((rows, width + -(-need // rows) * LANES), BF16)]
    return call(pack_kernel, "pack", outs, [kept, received, tokens], (), after)


def tokens_kernel(strip, *values, width):
    folded = jnp.concatenate(
        [strip[:, at : at + LANES] for at in range(width, strip.shape[1], LANES)]
    ).astype(F32)
    for k, value in enumerate(values):
        size = value.shape[1]
        value[...] = sum(unfold(folded, k + 2 * term, size) for term in range(3))


def tokens_of(strip, rows, width, after):
    outs = [shape((1, rows), F32)] * 2
    kernel = functools.partial(tokens_kernel, width=width)
    return call(kernel, "tokens_of", outs, [strip], (), after)


def finish_kernel(*refs, start, so_far):
    kept, received, out, token, source, done = refs[so_far:]
    source[...] = (kept[...].astype(F32) + received[...].astype(F32)).astype(BF16)
    token[...] = jnp.zeros(token.shape, F32)
    run_copies(copy_pairs(source, out.at[:, start : start + source.shape[1]]), done)


def finish(parts, dims, start, so_far, after):
    return call(
        functools.partial(finish_kernel, start=start, so_far=len(so_far)),
        "finish",
        [pltpu.HBM(dims, BF16), shape((8, LANES), F32)],
        list(parts),
        [pltpu.VMEM(parts[0].shape, BF16), pltpu.SemaphoreType.DMA((8,))],
        after,
        so_far,
        bool(so_far),
    )


def local(hidden, out_weight, teacher_logits, token_ids, loss_mask):
    rows, features = hidden.shape
    width = out_weight.shape[1]
    vocab_size = lax.axis_size("vocab")
    group_axes, group_size = ("role", "dp"), lax.axis_size("role") * lax.axis_size("dp")
    assert lax.axis_size("role") == 2 and lax.axis_size("dp") == 4
    assert vocab_size & (vocab_size - 1) == 0 and vocab_size >= QUARTERS

    ids, mask = token_ids.reshape(1, rows), loss_mask.reshape(1, rows)
    pieces = []
    for k, some in enumerate([[(0, 0)], [(0, 1)], [(1, 0), (1, 1)]]):
        pieces += pick_rows(hidden, some, (ids, mask) if k == 1 else (), after=pieces[-1:])
    direct = [xor_swap(piece, "role", 1) for piece in pieces]
    known = teacher_stats(teacher_logits, after=pieces[1:2])
    direct[0] = pass_on(direct[0], [known])
    direct[1], side = unpack_rows(direct[1], rows)
    count = count_rows(side, mask)
    count = sum_rows(count, xor_swap(count, "dp", 1))
    direct[3] = pass_on(direct[3], [count])
    counts = [count, xor_swap(count, "dp", 2)]
    other = [xor_swap(piece, "vocab", 1) for piece in direct]

    logits, hidden_t, stats = [], [], []
    for group in range(2):
        pair = slice(2 * group, 2 * group + 2)
        done = group_logits(
            direct[pair],
            other[pair],
            out_weight,
            teacher_logits,
            side,
            known,
            stats[-1:],
            after=counts[1:] if group else direct[3:],
        )
        for values, value in zip((logits, stats), done):
            values.append(value)
        hidden_t.append(turn_rows(direct[pair], other[pair], after=stats[group:]))
    chunks = column_chunks(width, (7, 6, 6))
    split = chunks[1][0]
    slopes, tokens, columns = first_slopes(
        over_vocab(stats[1], vocab_size), side, counts, teacher_logits, logits, split, hidden_t[1:]
    )
    ranges = [(0, list(slopes))]
    last = slopes[1]

    def slope_step(last):
        slopes = more_slopes(columns, teacher_logits, logits, split, width - split, after=[last])
        ranges.append((split, list(slopes)))
        return slopes[1]

    by_group = vocab_size == QUARTERS
    home, hidden_in = [], []

    def hidden_step(last):
        k = len(home)
        if k == 0 or by_group:
            some = [s[k : k + 1] if by_group else s for _, s in ranges]
            last, kept = hidden_blocks(some, out_weight, vocab_size, after=[last])
            home.append(kept)
            hidden_in.append(xor_swap(last, "vocab", 1))
        return last

    arrived, near = [], []

    def chunk_of(k):
        start, size = chunks[k]
        begin, slopes = ranges[min(k, 1)]
        return slopes, start - begin, size

    def away_step(last):
        last = weight_away(hidden_t, *chunk_of(len(arrived)), after=[last])
        arrived.append(exchange(last, group_axes, group_size, lambda i: i ^ 1))
        return last

    def near_step(last):
        k = len(near)
        slopes, start, _ = chunk_of(k)
        leaving, last = weight_home(hidden_t, slopes, arrived[k], start, after=[last])
        near.append((last, exchange(leaving, group_axes, group_size, near_of)))
        return last

    far, grad_weight, returned, outs = [], [], [], []

    def far_step(last):
        kept, received = near[len(far)]
        leaving, last = add(kept, received, 2, after=[last])
        far.append((last, exchange(leaving, group_axes, group_size, far_of)))
        return last

    def weight_step(last):
        k = len(grad_weight)
        dims = (features // group_size, width)
        result, last = finish(far[k], dims, chunks[k][0], grad_weight[-1:], [last])
        grad_weight.append(result)
        return last

    halved = []

    def halve_step(last):
        if len(halved) < len(home):
            k = len(halved)
            leaving, last = add(home[k], hidden_in[k], 2, after=[last])
            halved.append((last, xor_swap(leaving, "vocab", 2)))
        return last

    def return_step(last):
        if len(returned) < len(home):
            kept, received = halved[len(returned)]
            bit = 4
            while bit < vocab_size:
                leaving, last = add(kept, received, 2, after=[last])
                kept, received = last, xor_swap(leaving, "vocab", bit)
                bit *= 2
            if returned:
                (last,) = add(kept, received, 1, after=[last])
            else:
                (last,) = pack(kept, received, tokens, after=[last])
            returned.append(xor_swap(last, "role", 1))
        return last

    def tokens_step(last):
        outs.extend(tokens_of(returned[0], rows, features, [last]))
        return outs[0]

    steps = {
        "s": slope_step,
        "a": away_step,
        "n": near_step,
        "h": hidden_step,
        "f": far_step,
        "v": halve_step,
        "r": return_step,
        "w": weight_step,
        "t": tokens_step,
    }
    for name in "asaanhnnhfvrfvfwwrtw":
        last = steps[name](last)

    grad_hidden = jnp.concatenate([r[:, :features] for r in returned])
    return outs[0].reshape(rows), outs[1].reshape(rows), grad_hidden, grad_weight[-1]


def solution(mesh):
    return jax.shard_map(
        local,
        mesh=mesh,
        in_specs=(
            P(("role", "dp"), None),
            P(None, "vocab"),
            P(("role", "dp"), "vocab"),
            P(("role", "dp")),
            P(("role", "dp")),
        ),
        out_specs=(
            P(("role", "dp")),
            P(("role", "dp")),
            P(("role", "dp", "vocab"), None),
            P(("role", "dp"), "vocab"),
        ),
        check_vma=False,
    )
```

```python
import functools

import jax
import jax.numpy as jnp
from jax import lax
from jax.experimental import pallas as pl
from jax.experimental.pallas import tpu as pltpu
from jax.sharding import PartitionSpec as P

F32 = jnp.float32
BF16 = jnp.bfloat16
VMEM_LIMIT = 18 * 1024 * 1024
LANES = 128
STEP = 16
LONG = 20_000_000_000
COST = 2_000_000_000
DIGIT = 128
BAND = 32
STATS = 8
QUARTERS = 4


def exchange(array, axes, size, partner):
    return lax.ppermute(array, axes, [(i, partner(i)) for i in range(size)])


def xor_swap(array, axis, mask):
    return exchange(array, axis, lax.axis_size(axis), lambda i: i ^ mask)


def shape(dims, dtype):
    return jax.ShapeDtypeStruct(dims, dtype)


def call(kernel, name, outs, arrays, scratch=(), after=(), far=(), aliases=False, flops=1024):
    skip = len(after)
    on_chip = pl.BlockSpec(memory_space=pltpu.VMEM)
    in_hbm = pl.BlockSpec(memory_space=pltpu.HBM)
    return pl.pallas_call(
        lambda *refs: kernel(*refs[skip:]),
        in_specs=[pl.BlockSpec(memory_space=pl.ANY)] * (skip + len(far))
        + [on_chip] * len(arrays),
        out_specs=[on_chip if isinstance(o, jax.ShapeDtypeStruct) else in_hbm for o in outs],
        out_shape=outs,
        scratch_shapes=list(scratch),
        input_output_aliases={skip: 0} if aliases else {},
        compiler_params=pltpu.CompilerParams(vmem_limit_bytes=VMEM_LIMIT),
        cost_estimate=pl.CostEstimate(flops=flops, bytes_accessed=1024, transcendentals=0),
        name=name,
    )(*after, *far, *arrays)


def column_chunks(width, shares):
    bounds = [width // LANES * sum(shares[:i]) // sum(shares) for i in range(len(shares) + 1)]
    return [(a * LANES, (b - a) * LANES) for a, b in zip(bounds, bounds[1:])]


def tiles(start, size, step):
    return [(at, min(step, start + size - at)) for at in range(start, start + size, step)]


def spread(row):
    return jnp.broadcast_to(row, (LANES, row.shape[1])).T


def lane_sum(ref):
    return jnp.sum(ref[...].T, axis=0, keepdims=True)


def fold(row):
    return jnp.concatenate([row[:, at : at + LANES] for at in range(0, row.shape[1], LANES)])


def unfold(values, k, count):
    each = count // LANES
    rows = [values[k * each + i : k * each + i + 1] for i in range(each)]
    return jnp.concatenate(rows, axis=1)


def pad_rows(values, rows):
    return jnp.concatenate([values, jnp.zeros((rows - values.shape[0], LANES), values.dtype)])


def row_steps(total, group):
    block = total // QUARTERS
    inside = block // 2

    def at(i):
        quarter, rest = i * STEP // inside, i * STEP % inside
        here = pl.multiple_of(i * STEP, STEP)
        there = pl.multiple_of(quarter * block + group * inside + rest, STEP)
        return pl.ds(here, STEP), pl.ds(there, STEP)

    return at


def copy_pairs(source, target, parts=4):
    rows = source.shape[0]
    size = max(STEP, -(-rows // parts) // STEP * STEP)
    return [
        (source.at[at : min(at + size, rows), :], target.at[at : min(at + size, rows), :])
        for at in range(0, rows, size)
    ]


def run_copies(pairs, done):
    copies = [pltpu.make_async_copy(*pair, done.at[i]) for i, pair in enumerate(pairs)]
    for copy in copies:
        copy.start()
    for copy in copies:
        copy.wait()


def near_of(index):
    return index ^ (2 if index & 1 else 4)


def far_of(index):
    return index ^ (4 if index & 1 else 2)


def weight_order():
    me = lax.axis_index("role") * 4 + lax.axis_index("dp")
    order = []
    for index in (me ^ 1, me):
        near = 4 - 2 * (index & 1)
        far = 6 - near
        order += [index ^ near ^ far, index ^ near, index ^ far, index]
    return order


def hidden_order(vocab_size):
    order = [lax.axis_index("vocab")]
    bit = vocab_size // 2
    while bit:
        order = [o ^ bit for o in order] + order
        bit //= 2
    return order


def pick_kernel(hidden, *refs, pieces, extra):
    sources, refs = refs[:extra], refs[extra:]
    outs, refs = refs[: len(pieces)], refs[len(pieces) :]
    landed, done = refs[:-1], refs[-1]
    odd = lax.axis_index("vocab") & 1
    block = hidden.shape[0] // QUARTERS
    size = block // 2
    pairs = list(zip(sources, landed))
    for (group, k), out in zip(pieces, outs):
        at = pl.multiple_of((2 * odd + k) * block + group * size, size)
        pairs += copy_pairs(hidden.at[pl.ds(at, size), :], out.at[:, : hidden.shape[1]])
    run_copies(pairs, done)
    if extra:
        ids, mask = (ref[...] for ref in landed)
        rest, terms = ids, []
        for _ in range(3):
            terms.append(rest & (DIGIT - 1))
            rest = rest >> (DIGIT.bit_length() - 1)
        values = jnp.concatenate([fold(v) for v in (*terms, mask)])
        outs[0][:, outs[0].shape[1] - LANES :] = pad_rows(values.astype(F32), size).astype(BF16)


def pick_rows(hidden, pieces, extra=(), after=()):
    rows, features = hidden.shape
    size = rows // QUARTERS // 2
    far = [pltpu.with_memory_space_constraint(a, pltpu.HBM) for a in (hidden, *extra)]
    more = [LANES if extra and i == 0 else 0 for i in range(len(pieces))]
    return call(
        functools.partial(pick_kernel, pieces=pieces, extra=len(extra)),
        "pick_rows",
        [shape((size, features + n), BF16) for n in more],
        [],
        [pltpu.VMEM((1, rows), jnp.int32)] * len(extra)
        + [pltpu.SemaphoreType.DMA((4 * len(pieces) + len(extra),))],
        after,
        far,
        flops=LONG,
    )


def unpack_kernel(packed, piece, side):
    features, count = piece.shape[1], side.shape[1]
    piece[...] = packed[:, :features]
    values = packed[:, features:].astype(F32)
    digits = [unfold(values, k, count) for k in range(4)]
    side[0:1, :] = digits[0] + DIGIT * (digits[1] + DIGIT * digits[2])
    side[1:2, :] = digits[3]


def unpack_rows(packed, rows):
    dims = (packed.shape[0], packed.shape[1] - LANES)
    return call(
        unpack_kernel,
        "unpack_rows",
        [shape(dims, BF16), shape((2, rows), F32)],
        [packed],
    )


def teacher_kernel(teacher, out, top, total):
    rows, width = teacher.shape

    @pl.loop(0, rows // STEP, unroll=2)
    def _(i):
        at = pl.ds(pl.multiple_of(i * STEP, STEP), STEP)
        best = teacher[at, 0:LANES]
        for start, size in tiles(LANES, width - LANES, LANES):
            best = jnp.maximum(best, teacher[at, start : start + size])
        top[at, :] = best.astype(F32)

    top_row = jnp.max(top[...].T, axis=0, keepdims=True)
    top[...] = spread(top_row)

    @pl.loop(0, rows // STEP, unroll=2)
    def _(i):
        at = pl.ds(pl.multiple_of(i * STEP, STEP), STEP)
        shift = top[at, :]
        acc = jnp.zeros((STEP, LANES), F32)
        for start, size in tiles(0, width, LANES):
            acc += jnp.exp(teacher[at, start : start + size].astype(F32) - shift)
        total[at, :] = acc

    out[...] = jnp.concatenate(
        [jnp.zeros((3, rows), F32), top_row, lane_sum(total), jnp.zeros((3, rows), F32)]
    )


def teacher_stats(teacher, after=()):
    rows, width = teacher.shape
    return call(
        teacher_kernel,
        "teacher_stats",
        [shape((STATS, rows), F32)],
        [teacher],
        [pltpu.VMEM((rows, LANES), F32)] * 2,
        after,
        flops=LONG,
    )[0]


def pass_on(array, after):
    outs = [shape(array.shape, array.dtype)]
    return call(lambda *refs: None, "pass_on", outs, [], (), after, [array], True)[0]


def count_kernel(side, mask, out):
    total = jnp.sum(side[1:2, :]) + jnp.sum(mask[...].astype(F32))
    out[...] = jnp.full(out.shape, total)


def sum_kernel(first, second, out):
    out[...] = first[...] + second[...]


def count_rows(side, mask):
    return call(count_kernel, "count_rows", [shape((8, LANES), F32)], [side, mask])[0]


def sum_rows(first, second):
    return call(sum_kernel, "sum_rows", [shape((8, LANES), F32)], [first, second])[0]


def gather_rows(direct, other, rows_in):
    odd = lax.axis_index("vocab") & 1
    half = rows_in.shape[0] // 2
    for first, refs in ((odd, direct), (1 - odd, other)):
        for i, ref in enumerate(refs):
            count = ref.shape[0]
            at = pl.multiple_of(first * half + i * count, count)
            rows_in[pl.ds(at, count), :] = ref[...]


def turn_rows(direct, other, after=()):
    count = len(direct)
    rows, features = 2 * count * direct[0].shape[0], direct[0].shape[1]

    def kernel(*refs):
        out, rows_in, turned = refs[2 * count :]
        gather_rows(refs[:count], refs[count : 2 * count], rows_in)
        turned[...] = rows_in[...].T
        height = features // 8
        for i, block in enumerate(weight_order()):
            at = pl.ds(pl.multiple_of(block * height, STEP), height)
            out[i * height : (i + 1) * height, :] = turned[at, :]

    return call(
        kernel,
        "turn_rows",
        [shape((features, rows), BF16)],
        [*direct, *other],
        [pltpu.VMEM((rows, features), BF16), pltpu.VMEM((features, rows), BF16)],
        after,
    )[0]


def logits_kernel(direct, other, weight, teacher, side, known, *refs):
    group = len(refs) - 8
    first, refs = refs[:group], refs[group:]
    logits, stats, rows_in, top, total, gap, picked, chosen = refs
    rows, width = logits.shape
    vocab = lax.axis_index("vocab")
    gather_rows(direct, other, rows_in)
    value = rows_in[...]

    ids = side[0:1, :] - (vocab * width).astype(F32)
    chosen[...] = spread(ids) - lax.broadcasted_iota(jnp.int32, chosen.shape, 1).astype(F32)
    for ref in (total, gap, picked):
        ref[...] = jnp.zeros(ref.shape, F32)
    inside = rows // QUARTERS
    for start, size in tiles(0, width, 4 * LANES):
        tile = jnp.dot(value, weight[:, start : start + size], preferred_element_type=F32)
        logits[:, start : start + size] = tile
        columns = range(start, start + size, LANES)
        for at in range(0, rows, BAND):
            here = slice(at, at + BAND)
            from_row = (at // inside * 2 + group) * inside + at % inside
            there = slice(from_row, from_row + BAND)
            students = [tile[here, c - start : c - start + LANES] for c in columns]
            best = functools.reduce(jnp.maximum, students)
            if start:
                last = top[here, :]
                best = jnp.maximum(best, last)
                scale = jnp.exp(last - best)
                sums = [total[there, :] * scale, gap[there, :] * scale]
                hit = picked[there, :]
            else:
                sums, hit = [0.0, 0.0], 0.0
            top[here, :] = best
            wanted = chosen[there, :]
            for c, student in zip(columns, students):
                target = teacher[there, c : c + LANES].astype(F32)
                share = jnp.exp(student - best)
                sums = [sums[0] + share, sums[1] + share * (student - target)]
                hit = hit + jnp.where(wanted == c, student, 0.0)
            total[there, :], gap[there, :], picked[there, :] = *sums, hit

    top_row = jnp.max(top[...].T, axis=0, keepdims=True)
    whole_top = spread(top_row)
    for at in range(0, rows, inside):
        here = slice(at, at + inside)
        from_row = (at // inside * 2 + group) * inside
        there = slice(from_row, from_row + inside)
        scale = jnp.exp(top[here, :] - whole_top[here, :])
        total[there, :] = total[there, :] * scale
        gap[there, :] = gap[there, :] * scale
        top[here, :] = whole_top[here, :]

    rows_known = {k: lane_sum(ref) for k, ref in ((1, total), (2, gap), (5, picked))}
    for q in range(QUARTERS):
        at = (2 * q + group) * inside
        total[at : at + inside, :] = top[q * inside : (q + 1) * inside, :]
    rows_known[0] = total[...].T[0:1, :]
    stats[...] = known[...]
    for k, row in rows_known.items():
        if first:
            lane = lax.broadcasted_iota(jnp.int32, row.shape, 1)
            row = jnp.where((lane & inside) != 0, row, first[0][k : k + 1, :])
        stats[k : k + 1, :] = row


def group_logits(direct, other, weight, teacher, side, known, first, after=()):
    rows, width = teacher.shape
    features = weight.shape[0]
    count = len(direct)

    def kernel(*refs):
        logits_kernel(refs[:count], refs[count : 2 * count], *refs[2 * count :])

    return call(
        kernel,
        "group_logits",
        [
            shape((rows // 2, width), F32),
            shape((STATS, rows), F32),
        ],
        [*direct, *other, weight, teacher, side, known, *first],
        [pltpu.VMEM((rows // 2, features), BF16)]
        + [pltpu.VMEM((rows // 2, LANES), F32)]
        + [pltpu.VMEM((rows, LANES), F32)] * 4,
        after,
        flops=LONG if first else COST,
    )


def join(parts):
    top = functools.reduce(jnp.maximum, [p[0] for p in parts])
    teacher_top = functools.reduce(jnp.maximum, [p[3] for p in parts])
    scales = [jnp.exp(p[0] - top) for p in parts]
    total = sum(s * p[1] for s, p in zip(scales, parts))
    gap = sum(s * p[2] for s, p in zip(scales, parts))
    teacher_total = sum(jnp.exp(p[3] - teacher_top) * p[4] for p in parts)
    picked = sum(p[5] for p in parts)
    return top, total, gap, teacher_top, teacher_total, picked


def over_vocab(stats, size):
    parts, done = [stats], 1
    while done < size:
        if done > 1:
            joined = join([[p[k] for k in range(6)] for p in parts])
            parts = [jnp.stack(list(joined) + [joined[0]] * (STATS - 6))]
        radix = min(4, size // done)
        parts += [xor_swap(parts[0], "vocab", k * done) for k in range(1, radix)]
        done *= radix
    return parts


def row_kernel(stats, side, counts, tokens, lses, shifts, weights):
    top, total, gap, teacher_top, teacher_total, picked = join(
        [[s[k : k + 1, :] for k in range(6)] for s in stats]
    )
    lse = top + jnp.log(total)
    diff = lse - (teacher_top + jnp.log(teacher_total))
    kl = gap / total - diff
    tokens[...] = jnp.concatenate([kl, picked - lse])
    mask_total = counts[0][0:1, 0:1] + counts[1][0:1, 0:1]
    lses[...] = spread(lse)
    shifts[...] = spread(diff + kl)
    weights[...] = spread(side[1:2, :] / jnp.maximum(mask_total, 1.0))


def slope_kernel(lses, shifts, weights, teacher, *refs, start):
    for group, (logits, slope) in enumerate(zip(refs[:2], refs[2:])):
        rows, width = slope.shape
        steps = row_steps(2 * rows, group)

        @pl.loop(0, rows // STEP, unroll=4)
        def _(i):
            here, there = steps(i)
            lse, shift, weight = lses[there, :], shifts[there, :], weights[there, :]
            for at, size in tiles(0, width, LANES):
                student = logits[here, start + at : start + at + size]
                target = teacher[there, start + at : start + at + size].astype(F32)
                value = weight * jnp.exp(student - lse) * (student - target - shift)
                slope[here, at : at + size] = value.astype(BF16)


def first_slopes(stats, side, counts, teacher, logits, size, after=()):
    rows = teacher.shape[0]
    parts = len(stats)

    def kernel(*refs):
        before, (slope_0, slope_1, *after) = refs[: parts + 6], refs[parts + 6 :]
        side, first, second, teacher, *logits = before[parts:]
        row_kernel(before[:parts], side, (first, second), *after)
        slope_kernel(*after[1:], teacher, *logits, slope_0, slope_1, start=0)

    *slopes, tokens, lses, shifts, weights = call(
        kernel,
        "slopes",
        [shape((rows // 2, size), BF16)] * 2
        + [shape((2, rows), F32)]
        + [shape((rows, LANES), F32)] * 3,
        [*stats, side, *counts, teacher, *logits],
        (),
        after,
    )
    return slopes, tokens, (lses, shifts, weights)


def more_slopes(columns, teacher, logits, start, size, after=()):
    rows = teacher.shape[0]
    return call(
        functools.partial(slope_kernel, start=start),
        "slopes",
        [shape((rows // 2, size), BF16)] * 2,
        [*columns, teacher, *logits],
        (),
        after,
    )


def weight_blocks(hidden_t, slopes, first, count, start, size):
    return sum(
        jnp.dot(
            left[first : first + count, :],
            right[:, start : start + size],
            preferred_element_type=F32,
        )
        for left, right in zip(hidden_t, slopes)
    )


def weight_away_kernel(*refs, start):
    hidden_t, slopes, out = refs[:2], refs[2:4], refs[4]
    out[...] = weight_blocks(hidden_t, slopes, 0, out.shape[0], start, out.shape[1]).astype(BF16)


def weight_away(hidden_t, slopes, start, size, after=()):
    features = hidden_t[0].shape[0]
    return call(
        functools.partial(weight_away_kernel, start=start),
        "weight_away",
        [shape((features // 2, size), BF16)],
        [*hidden_t, *slopes],
        (),
        after,
    )[0]


def weight_home_kernel(*refs, start):
    hidden_t, slopes, received, outs = refs[:2], refs[2:4], refs[4], refs[5:]
    count, size = outs[0].shape
    for part, out in enumerate(outs):
        value = weight_blocks(hidden_t, slopes, (2 + part) * count, count, start, size)
        value += received[part * count : (part + 1) * count, :].astype(F32)
        out[...] = value.astype(BF16)


def weight_home(hidden_t, slopes, received, start, after=()):
    count, size = received.shape
    return call(
        functools.partial(weight_home_kernel, start=start),
        "weight_home",
        [shape((count // 2, size), BF16)] * 2,
        [*hidden_t, *slopes, received],
        (),
        after,
    )


def hidden_kernel(*refs, vocab_size, groups):
    *slopes, weight, away, home, rows = refs
    blocks = vocab_size
    height = rows.shape[0] // blocks
    begin = 0
    for at_part in range(0, len(slopes), groups):
        part = slopes[at_part : at_part + groups]
        columns = slice(begin, begin + part[0].shape[1])
        begin = columns.stop
        for i, block in enumerate(hidden_order(vocab_size)):
            to = slice(i * height, (i + 1) * height)
            if groups == 1:
                at = pl.multiple_of(block * height, height)
                rows[to, columns] = part[0][pl.ds(at, height), :]
                continue
            per = vocab_size // QUARTERS // 2
            at = pl.multiple_of((block // (2 * per) * per + block % per) * height, height)
            for group, slope in enumerate(part):

                @pl.when(block // per % 2 == group)
                def _():
                    rows[to, columns] = slope[pl.ds(at, height), :]

    value = rows[...]
    middle = away.shape[0]
    for start, size in tiles(0, weight.shape[0], 2 * LANES):
        at = slice(start, start + size)
        result = lax.dot_general(
            value, weight[at, :], (((1,), (1,)), ((), ())), preferred_element_type=F32
        )
        away[:, at] = result[:middle].astype(BF16)
        home[:, at] = result[middle:]


def hidden_blocks(slopes, weight, vocab_size, after=()):
    width = weight.shape[1]
    rows = sum(s.shape[0] for s in slopes[0])
    dims = (rows // 2, weight.shape[0])
    return call(
        functools.partial(hidden_kernel, vocab_size=vocab_size, groups=len(slopes[0])),
        "hidden_grad",
        [shape(dims, BF16), shape(dims, F32)],
        [*sum(slopes, []), weight],
        [pltpu.VMEM((rows, width), BF16)],
        after,
    )


def add_kernel(kept, received, *outs):
    count = outs[0].shape[0]
    for i, out in enumerate(outs):
        at = slice(i * count, (i + 1) * count)
        out[...] = (kept[at, :].astype(F32) + received[at, :].astype(F32)).astype(BF16)


def add(kept, received, parts, after=()):
    rows, width = kept.shape
    return call(
        add_kernel,
        "add",
        [shape((rows // parts, width), BF16)] * parts,
        [kept, received],
        (),
        after,
    )


def pack_kernel(kept, received, tokens, out):
    rows, width = kept.shape
    out[:, :width] = (kept[...].astype(F32) + received[...].astype(F32)).astype(BF16)
    rest, terms = tokens[...], []
    for _ in range(3):
        terms.append(rest.astype(BF16).astype(F32))
        rest = rest - terms[-1]
    rows_of = [fold(term[k : k + 1]) for term in terms for k in range(2)]
    room = rows * (out.shape[1] - width) // LANES
    values = pad_rows(jnp.concatenate(rows_of), room).astype(BF16)
    for i in range(room // rows):
        at = width + i * LANES
        out[:, at : at + LANES] = values[i * rows : (i + 1) * rows]


def pack(kept, received, tokens, after=()):
    rows, width = kept.shape
    need = 6 * tokens.shape[1] // LANES
    outs = [shape((rows, width + -(-need // rows) * LANES), BF16)]
    return call(pack_kernel, "pack", outs, [kept, received, tokens], (), after)


def tokens_kernel(strip, *values, width):
    folded = jnp.concatenate(
        [strip[:, at : at + LANES] for at in range(width, strip.shape[1], LANES)]
    ).astype(F32)
    for k, value in enumerate(values):
        size = value.shape[1]
        value[...] = sum(unfold(folded, k + 2 * term, size) for term in range(3))


def tokens_of(strip, rows, width, after):
    outs = [shape((1, rows), F32)] * 2
    kernel = functools.partial(tokens_kernel, width=width)
    return call(kernel, "tokens_of", outs, [strip], (), after)


def finish_kernel(*refs, start, so_far):
    kept, received, out, token, source, done = refs[so_far:]
    source[...] = (kept[...].astype(F32) + received[...].astype(F32)).astype(BF16)
    token[...] = jnp.zeros(token.shape, F32)
    run_copies(copy_pairs(source, out.at[:, start : start + source.shape[1]]), done)


def finish(parts, dims, start, so_far, after):
    return call(
        functools.partial(finish_kernel, start=start, so_far=len(so_far)),
        "finish",
        [pltpu.HBM(dims, BF16), shape((8, LANES), F32)],
        list(parts),
        [pltpu.VMEM(parts[0].shape, BF16), pltpu.SemaphoreType.DMA((8,))],
        after,
        so_far,
        bool(so_far),
    )


def local(hidden, out_weight, teacher_logits, token_ids, loss_mask):
    rows, features = hidden.shape
    width = out_weight.shape[1]
    vocab_size = lax.axis_size("vocab")
    group_axes, group_size = ("role", "dp"), lax.axis_size("role") * lax.axis_size("dp")
    assert lax.axis_size("role") == 2 and lax.axis_size("dp") == 4
    assert vocab_size & (vocab_size - 1) == 0 and vocab_size >= QUARTERS

    ids, mask = token_ids.reshape(1, rows), loss_mask.reshape(1, rows)
    pieces = []
    for k, some in enumerate([[(0, 0)], [(0, 1)], [(1, 0), (1, 1)]]):
        pieces += pick_rows(hidden, some, (ids, mask) if k == 1 else (), after=pieces[-1:])
    direct = [xor_swap(piece, "role", 1) for piece in pieces]
    known = teacher_stats(teacher_logits, after=pieces[1:2])
    direct[0] = pass_on(direct[0], [known])
    direct[1], side = unpack_rows(direct[1], rows)
    count = count_rows(side, mask)
    count = sum_rows(count, xor_swap(count, "dp", 1))
    direct[3] = pass_on(direct[3], [count])
    counts = [count, xor_swap(count, "dp", 2)]
    other = [xor_swap(piece, "vocab", 1) for piece in direct]

    logits, hidden_t, stats = [], [], []
    for group in range(2):
        pair = slice(2 * group, 2 * group + 2)
        done = group_logits(
            direct[pair],
            other[pair],
            out_weight,
            teacher_logits,
            side,
            known,
            stats[-1:],
            after=counts[1:] if group else direct[3:],
        )
        for values, value in zip((logits, stats), done):
            values.append(value)
        hidden_t.append(turn_rows(direct[pair], other[pair], after=stats[group:]))
    chunks = column_chunks(width, (7, 6, 6))
    split = chunks[1][0]
    slopes, tokens, columns = first_slopes(
        over_vocab(stats[1], vocab_size), side, counts, teacher_logits, logits, split, hidden_t[1:]
    )
    ranges = [(0, list(slopes))]
    last = slopes[1]

    def slope_step(last):
        slopes = more_slopes(columns, teacher_logits, logits, split, width - split, after=[last])
        ranges.append((split, list(slopes)))
        return slopes[1]

    by_group = vocab_size == QUARTERS
    home, hidden_in = [], []

    def hidden_step(last):
        k = len(home)
        if k == 0 or by_group:
            some = [s[k : k + 1] if by_group else s for _, s in ranges]
            last, kept = hidden_blocks(some, out_weight, vocab_size, after=[last])
            home.append(kept)
            hidden_in.append(xor_swap(last, "vocab", 1))
        return last

    arrived, near = [], []

    def chunk_of(k):
        start, size = chunks[k]
        begin, slopes = ranges[min(k, 1)]
        return slopes, start - begin, size

    def away_step(last):
        last = weight_away(hidden_t, *chunk_of(len(arrived)), after=[last])
        arrived.append(exchange(last, group_axes, group_size, lambda i: i ^ 1))
        return last

    def near_step(last):
        k = len(near)
        slopes, start, _ = chunk_of(k)
        leaving, last = weight_home(hidden_t, slopes, arrived[k], start, after=[last])
        near.append((last, exchange(leaving, group_axes, group_size, near_of)))
        return last

    far, grad_weight, returned, outs = [], [], [], []

    def far_step(last):
        kept, received = near[len(far)]
        leaving, last = add(kept, received, 2, after=[last])
        far.append((last, exchange(leaving, group_axes, group_size, far_of)))
        return last

    def weight_step(last):
        k = len(grad_weight)
        dims = (features // group_size, width)
        result, last = finish(far[k], dims, chunks[k][0], grad_weight[-1:], [last])
        grad_weight.append(result)
        return last

    halved = []

    def halve_step(last):
        if len(halved) < len(home):
            k = len(halved)
            leaving, last = add(home[k], hidden_in[k], 2, after=[last])
            halved.append((last, xor_swap(leaving, "vocab", 2)))
        return last

    def return_step(last):
        if len(returned) < len(home):
            kept, received = halved[len(returned)]
            bit = 4
            while bit < vocab_size:
                leaving, last = add(kept, received, 2, after=[last])
                kept, received = last, xor_swap(leaving, "vocab", bit)
                bit *= 2
            if returned:
                (last,) = add(kept, received, 1, after=[last])
            else:
                (last,) = pack(kept, received, tokens, after=[last])
            returned.append(xor_swap(last, "role", 1))
        return last

    def tokens_step(last):
        outs.extend(tokens_of(returned[0], rows, features, [last]))
        return outs[0]

    steps = {
        "s": slope_step,
        "a": away_step,
        "n": near_step,
        "h": hidden_step,
        "f": far_step,
        "v": halve_step,
        "r": return_step,
        "w": weight_step,
        "t": tokens_step,
    }
    for name in "asaanhnnhfvrfvfwwrtw":
        last = steps[name](last)

    grad_hidden = jnp.concatenate([r[:, :features] for r in returned])
    return outs[0].reshape(rows), outs[1].reshape(rows), grad_hidden, grad_weight[-1]


def solution(mesh):
    return jax.shard_map(
        local,
        mesh=mesh,
        in_specs=(
            P(("role", "dp"), None),
            P(None, "vocab"),
            P(("role", "dp"), "vocab"),
            P(("role", "dp")),
            P(("role", "dp")),
        ),
        out_specs=(
            P(("role", "dp")),
            P(("role", "dp")),
            P(("role", "dp", "vocab"), None),
            P(("role", "dp"), "vocab"),
        ),
        check_vma=False,
    )
```

```python
import functools

import jax
import jax.numpy as jnp
from jax import lax
from jax.experimental import pallas as pl
from jax.experimental.pallas import tpu as pltpu
from jax.sharding import PartitionSpec as P

F32 = jnp.float32
BF16 = jnp.bfloat16
VMEM_LIMIT = 18 * 1024 * 1024
LANES = 128
STEP = 16
LONG = 20_000_000_000
COST = 2_000_000_000
DIGIT = 128
BAND = 32
STATS = 8
QUARTERS = 4


def exchange(array, axes, size, partner):
    return lax.ppermute(array, axes, [(i, partner(i)) for i in range(size)])


def xor_swap(array, axis, mask):
    return exchange(array, axis, lax.axis_size(axis), lambda i: i ^ mask)


def shape(dims, dtype):
    return jax.ShapeDtypeStruct(dims, dtype)


def call(kernel, name, outs, arrays, scratch=(), after=(), far=(), aliases=False, flops=1024):
    skip = len(after)
    on_chip = pl.BlockSpec(memory_space=pltpu.VMEM)
    in_hbm = pl.BlockSpec(memory_space=pltpu.HBM)
    return pl.pallas_call(
        lambda *refs: kernel(*refs[skip:]),
        in_specs=[pl.BlockSpec(memory_space=pl.ANY)] * (skip + len(far))
        + [on_chip] * len(arrays),
        out_specs=[on_chip if isinstance(o, jax.ShapeDtypeStruct) else in_hbm for o in outs],
        out_shape=outs,
        scratch_shapes=list(scratch),
        input_output_aliases={skip: 0} if aliases else {},
        compiler_params=pltpu.CompilerParams(vmem_limit_bytes=VMEM_LIMIT),
        cost_estimate=pl.CostEstimate(flops=flops, bytes_accessed=1024, transcendentals=0),
        name=name,
    )(*after, *far, *arrays)


def column_chunks(width, shares):
    bounds = [width // LANES * sum(shares[:i]) // sum(shares) for i in range(len(shares) + 1)]
    return [(a * LANES, (b - a) * LANES) for a, b in zip(bounds, bounds[1:])]


def tiles(start, size, step):
    return [(at, min(step, start + size - at)) for at in range(start, start + size, step)]


def spread(row):
    return jnp.broadcast_to(row, (LANES, row.shape[1])).T


def lane_sum(ref):
    return jnp.sum(ref[...].T, axis=0, keepdims=True)


def fold(row):
    return jnp.concatenate([row[:, at : at + LANES] for at in range(0, row.shape[1], LANES)])


def unfold(values, k, count):
    each = count // LANES
    rows = [values[k * each + i : k * each + i + 1] for i in range(each)]
    return jnp.concatenate(rows, axis=1)


def pad_rows(values, rows):
    return jnp.concatenate([values, jnp.zeros((rows - values.shape[0], LANES), values.dtype)])


def row_steps(total, group):
    block = total // QUARTERS
    inside = block // 2

    def at(i):
        quarter, rest = i * STEP // inside, i * STEP % inside
        here = pl.multiple_of(i * STEP, STEP)
        there = pl.multiple_of(quarter * block + group * inside + rest, STEP)
        return pl.ds(here, STEP), pl.ds(there, STEP)

    return at


def copy_pairs(source, target, parts=4):
    rows = source.shape[0]
    size = max(STEP, -(-rows // parts) // STEP * STEP)
    return [
        (source.at[at : min(at + size, rows), :], target.at[at : min(at + size, rows), :])
        for at in range(0, rows, size)
    ]


def run_copies(pairs, done):
    copies = [pltpu.make_async_copy(*pair, done.at[i]) for i, pair in enumerate(pairs)]
    for copy in copies:
        copy.start()
    for copy in copies:
        copy.wait()


def near_of(index):
    return index ^ (2 if index & 1 else 4)


def far_of(index):
    return index ^ (4 if index & 1 else 2)


def weight_order():
    me = lax.axis_index("role") * 4 + lax.axis_index("dp")
    order = []
    for index in (me ^ 1, me):
        near = 4 - 2 * (index & 1)
        far = 6 - near
        order += [index ^ near ^ far, index ^ near, index ^ far, index]
    return order


def hidden_order(vocab_size):
    order = [lax.axis_index("vocab")]
    bit = vocab_size // 2
    while bit:
        order = [o ^ bit for o in order] + order
        bit //= 2
    return order


def pick_kernel(hidden, *refs, pieces, extra):
    sources, refs = refs[:extra], refs[extra:]
    outs, refs = refs[: len(pieces)], refs[len(pieces) :]
    landed, done = refs[:-1], refs[-1]
    odd = lax.axis_index("vocab") & 1
    block = hidden.shape[0] // QUARTERS
    size = block // 2
    pairs = list(zip(sources, landed))
    for (group, k), out in zip(pieces, outs):
        at = pl.multiple_of((2 * odd + k) * block + group * size, size)
        pairs += copy_pairs(hidden.at[pl.ds(at, size), :], out.at[:, : hidden.shape[1]])
    run_copies(pairs, done)
    if extra:
        ids, mask = (ref[...] for ref in landed)
        rest, terms = ids, []
        for _ in range(3):
            terms.append(rest & (DIGIT - 1))
            rest = rest >> (DIGIT.bit_length() - 1)
        values = jnp.concatenate([fold(v) for v in (*terms, mask)])
        outs[0][:, outs[0].shape[1] - LANES :] = pad_rows(values.astype(F32), size).astype(BF16)


def pick_rows(hidden, pieces, extra=(), after=()):
    rows, features = hidden.shape
    size = rows // QUARTERS // 2
    far = [pltpu.with_memory_space_constraint(a, pltpu.HBM) for a in (hidden, *extra)]
    more = [LANES if extra and i == 0 else 0 for i in range(len(pieces))]
    return call(
        functools.partial(pick_kernel, pieces=pieces, extra=len(extra)),
        "pick_rows",
        [shape((size, features + n), BF16) for n in more],
        [],
        [pltpu.VMEM((1, rows), jnp.int32)] * len(extra)
        + [pltpu.SemaphoreType.DMA((4 * len(pieces) + len(extra),))],
        after,
        far,
        flops=LONG,
    )


def unpack_kernel(packed, piece, side):
    features, count = piece.shape[1], side.shape[1]
    piece[...] = packed[:, :features]
    values = packed[:, features:].astype(F32)
    digits = [unfold(values, k, count) for k in range(4)]
    side[0:1, :] = digits[0] + DIGIT * (digits[1] + DIGIT * digits[2])
    side[1:2, :] = digits[3]


def unpack_rows(packed, rows):
    dims = (packed.shape[0], packed.shape[1] - LANES)
    return call(
        unpack_kernel,
        "unpack_rows",
        [shape(dims, BF16), shape((2, rows), F32)],
        [packed],
    )


def teacher_kernel(teacher, out, top, total):
    rows, width = teacher.shape

    @pl.loop(0, rows // STEP, unroll=2)
    def _(i):
        at = pl.ds(pl.multiple_of(i * STEP, STEP), STEP)
        best = teacher[at, 0:LANES]
        for start, size in tiles(LANES, width - LANES, LANES):
            best = jnp.maximum(best, teacher[at, start : start + size])
        top[at, :] = best.astype(F32)

    top_row = jnp.max(top[...].T, axis=0, keepdims=True)
    top[...] = spread(top_row)

    @pl.loop(0, rows // STEP, unroll=2)
    def _(i):
        at = pl.ds(pl.multiple_of(i * STEP, STEP), STEP)
        shift = top[at, :]
        acc = jnp.zeros((STEP, LANES), F32)
        for start, size in tiles(0, width, LANES):
            acc += jnp.exp(teacher[at, start : start + size].astype(F32) - shift)
        total[at, :] = acc

    out[...] = jnp.concatenate(
        [jnp.zeros((3, rows), F32), top_row, lane_sum(total), jnp.zeros((3, rows), F32)]
    )


def teacher_stats(teacher, after=()):
    rows, width = teacher.shape
    return call(
        teacher_kernel,
        "teacher_stats",
        [shape((STATS, rows), F32)],
        [teacher],
        [pltpu.VMEM((rows, LANES), F32)] * 2,
        after,
        flops=LONG,
    )[0]


def pass_on(array, after):
    outs = [shape(array.shape, array.dtype)]
    return call(lambda *refs: None, "pass_on", outs, [], (), after, [array], True)[0]


def count_kernel(side, mask, out):
    total = jnp.sum(side[1:2, :]) + jnp.sum(mask[...].astype(F32))
    out[...] = jnp.full(out.shape, total)


def sum_kernel(first, second, out):
    out[...] = first[...] + second[...]


def count_rows(side, mask):
    return call(count_kernel, "count_rows", [shape((8, LANES), F32)], [side, mask])[0]


def sum_rows(first, second):
    return call(sum_kernel, "sum_rows", [shape((8, LANES), F32)], [first, second])[0]


def gather_rows(direct, other, rows_in):
    odd = lax.axis_index("vocab") & 1
    half = rows_in.shape[0] // 2
    for first, refs in ((odd, direct), (1 - odd, other)):
        for i, ref in enumerate(refs):
            count = ref.shape[0]
            at = pl.multiple_of(first * half + i * count, count)
            rows_in[pl.ds(at, count), :] = ref[...]


def turn_rows(direct, other, after=()):
    count = len(direct)
    rows, features = 2 * count * direct[0].shape[0], direct[0].shape[1]

    def kernel(*refs):
        out, rows_in, turned = refs[2 * count :]
        gather_rows(refs[:count], refs[count : 2 * count], rows_in)
        turned[...] = rows_in[...].T
        height = features // 8
        for i, block in enumerate(weight_order()):
            at = pl.ds(pl.multiple_of(block * height, STEP), height)
            out[i * height : (i + 1) * height, :] = turned[at, :]

    return call(
        kernel,
        "turn_rows",
        [shape((features, rows), BF16)],
        [*direct, *other],
        [pltpu.VMEM((rows, features), BF16), pltpu.VMEM((features, rows), BF16)],
        after,
    )[0]


def logits_kernel(direct, other, weight, teacher, side, known, *refs):
    group = len(refs) - 8
    first, refs = refs[:group], refs[group:]
    logits, stats, rows_in, top, total, gap, picked, chosen = refs
    rows, width = logits.shape
    vocab = lax.axis_index("vocab")
    gather_rows(direct, other, rows_in)
    value = rows_in[...]

    ids = side[0:1, :] - (vocab * width).astype(F32)
    chosen[...] = spread(ids) - lax.broadcasted_iota(jnp.int32, chosen.shape, 1).astype(F32)
    for ref in (total, gap, picked):
        ref[...] = jnp.zeros(ref.shape, F32)
    inside = rows // QUARTERS
    for start, size in tiles(0, width, 4 * LANES):
        tile = jnp.dot(value, weight[:, start : start + size], preferred_element_type=F32)
        logits[:, start : start + size] = tile
        columns = range(start, start + size, LANES)
        for at in range(0, rows, BAND):
            here = slice(at, at + BAND)
            from_row = (at // inside * 2 + group) * inside + at % inside
            there = slice(from_row, from_row + BAND)
            students = [tile[here, c - start : c - start + LANES] for c in columns]
            best = functools.reduce(jnp.maximum, students)
            if start:
                last = top[here, :]
                best = jnp.maximum(best, last)
                scale = jnp.exp(last - best)
                sums = [total[there, :] * scale, gap[there, :] * scale]
                hit = picked[there, :]
            else:
                sums, hit = [0.0, 0.0], 0.0
            top[here, :] = best
            wanted = chosen[there, :]
            for c, student in zip(columns, students):
                target = teacher[there, c : c + LANES].astype(F32)
                share = jnp.exp(student - best)
                sums = [sums[0] + share, sums[1] + share * (student - target)]
                hit = hit + jnp.where(wanted == c, student, 0.0)
            total[there, :], gap[there, :], picked[there, :] = *sums, hit

    top_row = jnp.max(top[...].T, axis=0, keepdims=True)
    whole_top = spread(top_row)
    for at in range(0, rows, inside):
        here = slice(at, at + inside)
        from_row = (at // inside * 2 + group) * inside
        there = slice(from_row, from_row + inside)
        scale = jnp.exp(top[here, :] - whole_top[here, :])
        total[there, :] = total[there, :] * scale
        gap[there, :] = gap[there, :] * scale
        top[here, :] = whole_top[here, :]

    rows_known = {k: lane_sum(ref) for k, ref in ((1, total), (2, gap), (5, picked))}
    for q in range(QUARTERS):
        at = (2 * q + group) * inside
        total[at : at + inside, :] = top[q * inside : (q + 1) * inside, :]
    rows_known[0] = total[...].T[0:1, :]
    stats[...] = known[...]
    for k, row in rows_known.items():
        if first:
            lane = lax.broadcasted_iota(jnp.int32, row.shape, 1)
            row = jnp.where((lane & inside) != 0, row, first[0][k : k + 1, :])
        stats[k : k + 1, :] = row


def group_logits(direct, other, weight, teacher, side, known, first, after=()):
    rows, width = teacher.shape
    features = weight.shape[0]
    count = len(direct)

    def kernel(*refs):
        logits_kernel(refs[:count], refs[count : 2 * count], *refs[2 * count :])

    return call(
        kernel,
        "group_logits",
        [
            shape((rows // 2, width), F32),
            shape((STATS, rows), F32),
        ],
        [*direct, *other, weight, teacher, side, known, *first],
        [pltpu.VMEM((rows // 2, features), BF16)]
        + [pltpu.VMEM((rows // 2, LANES), F32)]
        + [pltpu.VMEM((rows, LANES), F32)] * 4,
        after,
        flops=LONG if first else COST,
    )


def join(parts):
    top = functools.reduce(jnp.maximum, [p[0] for p in parts])
    teacher_top = functools.reduce(jnp.maximum, [p[3] for p in parts])
    scales = [jnp.exp(p[0] - top) for p in parts]
    total = sum(s * p[1] for s, p in zip(scales, parts))
    gap = sum(s * p[2] for s, p in zip(scales, parts))
    teacher_total = sum(jnp.exp(p[3] - teacher_top) * p[4] for p in parts)
    picked = sum(p[5] for p in parts)
    return top, total, gap, teacher_top, teacher_total, picked


def over_vocab(stats, size):
    parts, done = [stats], 1
    while done < size:
        if done > 1:
            joined = join([[p[k] for k in range(6)] for p in parts])
            parts = [jnp.stack(list(joined) + [joined[0]] * (STATS - 6))]
        radix = min(4, size // done)
        parts += [xor_swap(parts[0], "vocab", k * done) for k in range(1, radix)]
        done *= radix
    return parts


def row_kernel(stats, side, counts, tokens, lses, shifts, weights):
    top, total, gap, teacher_top, teacher_total, picked = join(
        [[s[k : k + 1, :] for k in range(6)] for s in stats]
    )
    lse = top + jnp.log(total)
    diff = lse - (teacher_top + jnp.log(teacher_total))
    kl = gap / total - diff
    tokens[...] = jnp.concatenate([kl, picked - lse])
    mask_total = counts[0][0:1, 0:1] + counts[1][0:1, 0:1]
    lses[...] = spread(lse)
    shifts[...] = spread(diff + kl)
    weights[...] = spread(side[1:2, :] / jnp.maximum(mask_total, 1.0))


def slope_kernel(lses, shifts, weights, teacher, *refs, start):
    for group, (logits, slope) in enumerate(zip(refs[:2], refs[2:])):
        rows, width = slope.shape
        steps = row_steps(2 * rows, group)

        @pl.loop(0, rows // STEP, unroll=4)
        def _(i):
            here, there = steps(i)
            lse, shift, weight = lses[there, :], shifts[there, :], weights[there, :]
            for at, size in tiles(0, width, LANES):
                student = logits[here, start + at : start + at + size]
                target = teacher[there, start + at : start + at + size].astype(F32)
                value = weight * jnp.exp(student - lse) * (student - target - shift)
                slope[here, at : at + size] = value.astype(BF16)


def first_slopes(stats, side, counts, teacher, logits, hidden_t, size):
    rows = teacher.shape[0]
    features = hidden_t[0].shape[0]
    parts = len(stats)

    def kernel(*refs):
        before, (away, slope_0, slope_1, *after) = refs[: parts + 8], refs[parts + 8 :]
        side, first, second, teacher, *logits = before[parts : parts + 6]
        row_kernel(before[:parts], side, (first, second), *after)
        slope_kernel(*after[1:], teacher, *logits, slope_0, slope_1, start=0)
        weight_away_kernel(*before[parts + 6 :], slope_0, slope_1, away, start=0)

    away, *slopes, tokens, lses, shifts, weights = call(
        kernel,
        "slopes",
        [shape((features // 2, size), BF16)]
        + [shape((rows // 2, size), BF16)] * 2
        + [shape((2, rows), F32)]
        + [shape((rows, LANES), F32)] * 3,
        [*stats, side, *counts, teacher, *logits, *hidden_t],
    )
    return away, slopes, tokens, (lses, shifts, weights)


def more_slopes(columns, teacher, logits, start, size, after=()):
    rows = teacher.shape[0]
    return call(
        functools.partial(slope_kernel, start=start),
        "slopes",
        [shape((rows // 2, size), BF16)] * 2,
        [*columns, teacher, *logits],
        (),
        after,
    )


def weight_blocks(hidden_t, slopes, first, count, start, size):
    return sum(
        jnp.dot(
            left[first : first + count, :],
            right[:, start : start + size],
            preferred_element_type=F32,
        )
        for left, right in zip(hidden_t, slopes)
    )


def weight_away_kernel(*refs, start):
    hidden_t, slopes, out = refs[:2], refs[2:4], refs[4]
    out[...] = weight_blocks(hidden_t, slopes, 0, out.shape[0], start, out.shape[1]).astype(BF16)


def weight_away(hidden_t, slopes, start, size, after=()):
    features = hidden_t[0].shape[0]
    return call(
        functools.partial(weight_away_kernel, start=start),
        "weight_away",
        [shape((features // 2, size), BF16)],
        [*hidden_t, *slopes],
        (),
        after,
    )[0]


def weight_home_kernel(*refs, start):
    hidden_t, slopes, received, outs = refs[:2], refs[2:4], refs[4], refs[5:]
    count, size = outs[0].shape
    for part, out in enumerate(outs):
        value = weight_blocks(hidden_t, slopes, (2 + part) * count, count, start, size)
        value += received[part * count : (part + 1) * count, :].astype(F32)
        out[...] = value.astype(BF16)


def weight_home(hidden_t, slopes, received, start, after=()):
    count, size = received.shape
    return call(
        functools.partial(weight_home_kernel, start=start),
        "weight_home",
        [shape((count // 2, size), BF16)] * 2,
        [*hidden_t, *slopes, received],
        (),
        after,
    )


def hidden_kernel(*refs, vocab_size, groups):
    *slopes, weight, away, home, rows = refs
    blocks = vocab_size
    height = rows.shape[0] // blocks
    begin = 0
    for at_part in range(0, len(slopes), groups):
        part = slopes[at_part : at_part + groups]
        columns = slice(begin, begin + part[0].shape[1])
        begin = columns.stop
        for i, block in enumerate(hidden_order(vocab_size)):
            to = slice(i * height, (i + 1) * height)
            if groups == 1:
                at = pl.multiple_of(block * height, height)
                rows[to, columns] = part[0][pl.ds(at, height), :]
                continue
            per = vocab_size // QUARTERS // 2
            at = pl.multiple_of((block // (2 * per) * per + block % per) * height, height)
            for group, slope in enumerate(part):

                @pl.when(block // per % 2 == group)
                def _():
                    rows[to, columns] = slope[pl.ds(at, height), :]

    value = rows[...]
    middle = away.shape[0]
    for start, size in tiles(0, weight.shape[0], 2 * LANES):
        at = slice(start, start + size)
        result = lax.dot_general(
            value, weight[at, :], (((1,), (1,)), ((), ())), preferred_element_type=F32
        )
        away[:, at] = result[:middle].astype(BF16)
        home[:, at] = result[middle:]


def hidden_blocks(slopes, weight, vocab_size, after=()):
    width = weight.shape[1]
    rows = sum(s.shape[0] for s in slopes[0])
    dims = (rows // 2, weight.shape[0])
    return call(
        functools.partial(hidden_kernel, vocab_size=vocab_size, groups=len(slopes[0])),
        "hidden_grad",
        [shape(dims, BF16), shape(dims, F32)],
        [*sum(slopes, []), weight],
        [pltpu.VMEM((rows, width), BF16)],
        after,
    )


def add_kernel(kept, received, *outs):
    count = outs[0].shape[0]
    for i, out in enumerate(outs):
        at = slice(i * count, (i + 1) * count)
        out[...] = (kept[at, :].astype(F32) + received[at, :].astype(F32)).astype(BF16)


def add(kept, received, parts, after=()):
    rows, width = kept.shape
    return call(
        add_kernel,
        "add",
        [shape((rows // parts, width), BF16)] * parts,
        [kept, received],
        (),
        after,
    )


def pack_kernel(kept, received, tokens, out):
    rows, width = kept.shape
    out[:, :width] = (kept[...].astype(F32) + received[...].astype(F32)).astype(BF16)
    rest, terms = tokens[...], []
    for _ in range(3):
        terms.append(rest.astype(BF16).astype(F32))
        rest = rest - terms[-1]
    rows_of = [fold(term[k : k + 1]) for term in terms for k in range(2)]
    room = rows * (out.shape[1] - width) // LANES
    values = pad_rows(jnp.concatenate(rows_of), room).astype(BF16)
    for i in range(room // rows):
        at = width + i * LANES
        out[:, at : at + LANES] = values[i * rows : (i + 1) * rows]


def pack(kept, received, tokens, after=()):
    rows, width = kept.shape
    need = 6 * tokens.shape[1] // LANES
    outs = [shape((rows, width + -(-need // rows) * LANES), BF16)]
    return call(pack_kernel, "pack", outs, [kept, received, tokens], (), after)


def tokens_kernel(strip, *values, width):
    folded = jnp.concatenate(
        [strip[:, at : at + LANES] for at in range(width, strip.shape[1], LANES)]
    ).astype(F32)
    for k, value in enumerate(values):
        size = value.shape[1]
        value[...] = sum(unfold(folded, k + 2 * term, size) for term in range(3))


def tokens_of(strip, rows, width, after):
    outs = [shape((1, rows), F32)] * 2
    kernel = functools.partial(tokens_kernel, width=width)
    return call(kernel, "tokens_of", outs, [strip], (), after)


def finish_kernel(*refs, start, so_far):
    kept, received, out, token, source, done = refs[so_far:]
    source[...] = (kept[...].astype(F32) + received[...].astype(F32)).astype(BF16)
    token[...] = jnp.zeros(token.shape, F32)
    run_copies(copy_pairs(source, out.at[:, start : start + source.shape[1]]), done)


def finish(parts, dims, start, so_far, after):
    return call(
        functools.partial(finish_kernel, start=start, so_far=len(so_far)),
        "finish",
        [pltpu.HBM(dims, BF16), shape((8, LANES), F32)],
        list(parts),
        [pltpu.VMEM(parts[0].shape, BF16), pltpu.SemaphoreType.DMA((8,))],
        after,
        so_far,
        bool(so_far),
    )


def local(hidden, out_weight, teacher_logits, token_ids, loss_mask):
    rows, features = hidden.shape
    width = out_weight.shape[1]
    vocab_size = lax.axis_size("vocab")
    group_axes, group_size = ("role", "dp"), lax.axis_size("role") * lax.axis_size("dp")
    assert lax.axis_size("role") == 2 and lax.axis_size("dp") == 4
    assert vocab_size & (vocab_size - 1) == 0 and vocab_size >= QUARTERS

    ids, mask = token_ids.reshape(1, rows), loss_mask.reshape(1, rows)
    pieces = []
    for k, some in enumerate([[(0, 0)], [(0, 1)], [(1, 0), (1, 1)]]):
        pieces += pick_rows(hidden, some, (ids, mask) if k == 1 else (), after=pieces[-1:])
    direct = [xor_swap(piece, "role", 1) for piece in pieces]
    known = teacher_stats(teacher_logits, after=pieces[1:2])
    direct[0] = pass_on(direct[0], [known])
    direct[1], side = unpack_rows(direct[1], rows)
    count = count_rows(side, mask)
    count = sum_rows(count, xor_swap(count, "dp", 1))
    direct[3] = pass_on(direct[3], [count])
    counts = [count, xor_swap(count, "dp", 2)]
    other = [xor_swap(piece, "vocab", 1) for piece in direct]

    logits, hidden_t, stats = [], [], []
    for group in range(2):
        pair = slice(2 * group, 2 * group + 2)
        done = group_logits(
            direct[pair],
            other[pair],
            out_weight,
            teacher_logits,
            side,
            known,
            stats[-1:],
            after=counts[1:] if group else direct[3:],
        )
        for values, value in zip((logits, stats), done):
            values.append(value)
        hidden_t.append(turn_rows(direct[pair], other[pair], after=stats[group:]))
    chunks = column_chunks(width, (7, 6, 6))
    split = chunks[1][0]
    last, slopes, tokens, columns = first_slopes(
        over_vocab(stats[1], vocab_size), side, counts, teacher_logits, logits, hidden_t, split
    )
    ranges = [(0, list(slopes))]

    def slope_step(last):
        slopes = more_slopes(columns, teacher_logits, logits, split, width - split, after=[last])
        ranges.append((split, list(slopes)))
        return slopes[1]

    by_group = vocab_size == QUARTERS
    home, hidden_in = [], []

    def hidden_step(last):
        k = len(home)
        if k == 0 or by_group:
            some = [s[k : k + 1] if by_group else s for _, s in ranges]
            last, kept = hidden_blocks(some, out_weight, vocab_size, after=[last])
            home.append(kept)
            hidden_in.append(xor_swap(last, "vocab", 1))
        return last

    arrived, near = [], []

    def chunk_of(k):
        start, size = chunks[k]
        begin, slopes = ranges[min(k, 1)]
        return slopes, start - begin, size

    def away_step(last):
        if arrived:
            last = weight_away(hidden_t, *chunk_of(len(arrived)), after=[last])
        arrived.append(exchange(last, group_axes, group_size, lambda i: i ^ 1))
        return last

    def near_step(last):
        k = len(near)
        slopes, start, _ = chunk_of(k)
        leaving, last = weight_home(hidden_t, slopes, arrived[k], start, after=[last])
        near.append((last, exchange(leaving, group_axes, group_size, near_of)))
        return last

    far, grad_weight, returned, outs = [], [], [], []

    def far_step(last):
        kept, received = near[len(far)]
        leaving, last = add(kept, received, 2, after=[last])
        far.append((last, exchange(leaving, group_axes, group_size, far_of)))
        return last

    def weight_step(last):
        k = len(grad_weight)
        dims = (features // group_size, width)
        result, last = finish(far[k], dims, chunks[k][0], grad_weight[-1:], [last])
        grad_weight.append(result)
        return last

    halved = []

    def halve_step(last):
        if len(halved) < len(home):
            k = len(halved)
            leaving, last = add(home[k], hidden_in[k], 2, after=[last])
            halved.append((last, xor_swap(leaving, "vocab", 2)))
        return last

    def return_step(last):
        if len(returned) < len(home):
            kept, received = halved[len(returned)]
            bit = 4
            while bit < vocab_size:
                leaving, last = add(kept, received, 2, after=[last])
                kept, received = last, xor_swap(leaving, "vocab", bit)
                bit *= 2
            if returned:
                (last,) = add(kept, received, 1, after=[last])
            else:
                (last,) = pack(kept, received, tokens, after=[last])
            returned.append(xor_swap(last, "role", 1))
        return last

    def tokens_step(last):
        outs.extend(tokens_of(returned[0], rows, features, [last]))
        return outs[0]

    steps = {
        "s": slope_step,
        "a": away_step,
        "n": near_step,
        "h": hidden_step,
        "f": far_step,
        "v": halve_step,
        "r": return_step,
        "w": weight_step,
        "t": tokens_step,
    }
    for name in "asaanhnnhfvrfvfwwrtw":
        last = steps[name](last)

    grad_hidden = jnp.concatenate([r[:, :features] for r in returned])
    return outs[0].reshape(rows), outs[1].reshape(rows), grad_hidden, grad_weight[-1]


def solution(mesh):
    return jax.shard_map(
        local,
        mesh=mesh,
        in_specs=(
            P(("role", "dp"), None),
            P(None, "vocab"),
            P(("role", "dp"), "vocab"),
            P(("role", "dp")),
            P(("role", "dp")),
        ),
        out_specs=(
            P(("role", "dp")),
            P(("role", "dp")),
            P(("role", "dp", "vocab"), None),
            P(("role", "dp"), "vocab"),
        ),
        check_vma=False,
    )
```

```python
import functools

import jax
import jax.numpy as jnp
from jax import lax
from jax.experimental import pallas as pl
from jax.experimental.pallas import tpu as pltpu
from jax.sharding import PartitionSpec as P

F32 = jnp.float32
BF16 = jnp.bfloat16
VMEM_LIMIT = 18 * 1024 * 1024
LANES = 128
STEP = 16
LONG = 20_000_000_000
COST = 2_000_000_000
DIGIT = 128
BAND = 32
STATS = 8
QUARTERS = 4


def exchange(array, axes, size, partner):
    return lax.ppermute(array, axes, [(i, partner(i)) for i in range(size)])


def xor_swap(array, axis, mask):
    return exchange(array, axis, lax.axis_size(axis), lambda i: i ^ mask)


def shape(dims, dtype):
    return jax.ShapeDtypeStruct(dims, dtype)


def call(kernel, name, outs, arrays, scratch=(), after=(), far=(), aliases=False, flops=1024):
    skip = len(after)
    on_chip = pl.BlockSpec(memory_space=pltpu.VMEM)
    in_hbm = pl.BlockSpec(memory_space=pltpu.HBM)
    return pl.pallas_call(
        lambda *refs: kernel(*refs[skip:]),
        in_specs=[pl.BlockSpec(memory_space=pl.ANY)] * (skip + len(far))
        + [on_chip] * len(arrays),
        out_specs=[on_chip if isinstance(o, jax.ShapeDtypeStruct) else in_hbm for o in outs],
        out_shape=outs,
        scratch_shapes=list(scratch),
        input_output_aliases={skip: 0} if aliases else {},
        compiler_params=pltpu.CompilerParams(vmem_limit_bytes=VMEM_LIMIT),
        cost_estimate=pl.CostEstimate(flops=flops, bytes_accessed=1024, transcendentals=0),
        name=name,
    )(*after, *far, *arrays)


def column_chunks(width, shares):
    bounds = [width // LANES * sum(shares[:i]) // sum(shares) for i in range(len(shares) + 1)]
    return [(a * LANES, (b - a) * LANES) for a, b in zip(bounds, bounds[1:])]


def tiles(start, size, step):
    return [(at, min(step, start + size - at)) for at in range(start, start + size, step)]


def spread(row):
    return jnp.broadcast_to(row, (LANES, row.shape[1])).T


def lane_sum(ref):
    return jnp.sum(ref[...].T, axis=0, keepdims=True)


def fold(row):
    return jnp.concatenate([row[:, at : at + LANES] for at in range(0, row.shape[1], LANES)])


def unfold(values, k, count):
    each = count // LANES
    rows = [values[k * each + i : k * each + i + 1] for i in range(each)]
    return jnp.concatenate(rows, axis=1)


def pad_rows(values, rows):
    return jnp.concatenate([values, jnp.zeros((rows - values.shape[0], LANES), values.dtype)])


def row_steps(total, group):
    block = total // QUARTERS
    inside = block // 2

    def at(i):
        quarter, rest = i * STEP // inside, i * STEP % inside
        here = pl.multiple_of(i * STEP, STEP)
        there = pl.multiple_of(quarter * block + group * inside + rest, STEP)
        return pl.ds(here, STEP), pl.ds(there, STEP)

    return at


def copy_pairs(source, target, parts=4):
    rows = source.shape[0]
    size = max(STEP, -(-rows // parts) // STEP * STEP)
    return [
        (source.at[at : min(at + size, rows), :], target.at[at : min(at + size, rows), :])
        for at in range(0, rows, size)
    ]


def run_copies(pairs, done):
    copies = [pltpu.make_async_copy(*pair, done.at[i]) for i, pair in enumerate(pairs)]
    for copy in copies:
        copy.start()
    for copy in copies:
        copy.wait()


def near_of(index):
    return index ^ (2 if index & 1 else 4)


def far_of(index):
    return index ^ (4 if index & 1 else 2)


def weight_order():
    me = lax.axis_index("role") * 4 + lax.axis_index("dp")
    order = []
    for index in (me ^ 1, me):
        near = 4 - 2 * (index & 1)
        far = 6 - near
        order += [index ^ near ^ far, index ^ near, index ^ far, index]
    return order


def hidden_order(vocab_size):
    order = [lax.axis_index("vocab")]
    bit = vocab_size // 2
    while bit:
        order = [o ^ bit for o in order] + order
        bit //= 2
    return order


def pick_kernel(hidden, *refs, pieces, extra):
    sources, refs = refs[:extra], refs[extra:]
    outs, refs = refs[: len(pieces)], refs[len(pieces) :]
    landed, done = refs[:-1], refs[-1]
    odd = lax.axis_index("vocab") & 1
    block = hidden.shape[0] // QUARTERS
    size = block // 2
    pairs = list(zip(sources, landed))
    for (group, k), out in zip(pieces, outs):
        at = pl.multiple_of((2 * odd + k) * block + group * size, size)
        pairs += copy_pairs(hidden.at[pl.ds(at, size), :], out.at[:, : hidden.shape[1]])
    run_copies(pairs, done)
    if extra:
        ids, mask = (ref[...] for ref in landed)
        rest, terms = ids, []
        for _ in range(3):
            terms.append(rest & (DIGIT - 1))
            rest = rest >> (DIGIT.bit_length() - 1)
        values = jnp.concatenate([fold(v) for v in (*terms, mask)])
        outs[0][:, outs[0].shape[1] - LANES :] = pad_rows(values.astype(F32), size).astype(BF16)


def pick_rows(hidden, pieces, extra=(), after=()):
    rows, features = hidden.shape
    size = rows // QUARTERS // 2
    far = [pltpu.with_memory_space_constraint(a, pltpu.HBM) for a in (hidden, *extra)]
    more = [LANES if extra and i == 0 else 0 for i in range(len(pieces))]
    return call(
        functools.partial(pick_kernel, pieces=pieces, extra=len(extra)),
        "pick_rows",
        [shape((size, features + n), BF16) for n in more],
        [],
        [pltpu.VMEM((1, rows), jnp.int32)] * len(extra)
        + [pltpu.SemaphoreType.DMA((4 * len(pieces) + len(extra),))],
        after,
        far,
        flops=LONG,
    )


def unpack_kernel(packed, piece, side):
    features, count = piece.shape[1], side.shape[1]
    piece[...] = packed[:, :features]
    values = packed[:, features:].astype(F32)
    digits = [unfold(values, k, count) for k in range(4)]
    side[0:1, :] = digits[0] + DIGIT * (digits[1] + DIGIT * digits[2])
    side[1:2, :] = digits[3]


def unpack_rows(packed, rows):
    dims = (packed.shape[0], packed.shape[1] - LANES)
    return call(
        unpack_kernel,
        "unpack_rows",
        [shape(dims, BF16), shape((2, rows), F32)],
        [packed],
    )


def teacher_kernel(teacher, out, top, total):
    rows, width = teacher.shape

    @pl.loop(0, rows // STEP, unroll=2)
    def _(i):
        at = pl.ds(pl.multiple_of(i * STEP, STEP), STEP)
        best = teacher[at, 0:LANES]
        for start, size in tiles(LANES, width - LANES, LANES):
            best = jnp.maximum(best, teacher[at, start : start + size])
        top[at, :] = best.astype(F32)

    top_row = jnp.max(top[...].T, axis=0, keepdims=True)
    top[...] = spread(top_row)

    @pl.loop(0, rows // STEP, unroll=2)
    def _(i):
        at = pl.ds(pl.multiple_of(i * STEP, STEP), STEP)
        shift = top[at, :]
        acc = jnp.zeros((STEP, LANES), F32)
        for start, size in tiles(0, width, LANES):
            acc += jnp.exp(teacher[at, start : start + size].astype(F32) - shift)
        total[at, :] = acc

    out[...] = jnp.concatenate(
        [jnp.zeros((3, rows), F32), top_row, lane_sum(total), jnp.zeros((3, rows), F32)]
    )


def teacher_stats(teacher, after=()):
    rows, width = teacher.shape
    return call(
        teacher_kernel,
        "teacher_stats",
        [shape((STATS, rows), F32)],
        [teacher],
        [pltpu.VMEM((rows, LANES), F32)] * 2,
        after,
        flops=LONG,
    )[0]


def pass_on(array, after):
    outs = [shape(array.shape, array.dtype)]
    return call(lambda *refs: None, "pass_on", outs, [], (), after, [array], True)[0]


def count_kernel(side, mask, out):
    total = jnp.sum(side[1:2, :]) + jnp.sum(mask[...].astype(F32))
    out[...] = jnp.full(out.shape, total)


def sum_kernel(first, second, out):
    out[...] = first[...] + second[...]


def count_rows(side, mask):
    return call(count_kernel, "count_rows", [shape((8, LANES), F32)], [side, mask])[0]


def sum_rows(first, second):
    return call(sum_kernel, "sum_rows", [shape((8, LANES), F32)], [first, second])[0]


def gather_rows(direct, other, rows_in):
    odd = lax.axis_index("vocab") & 1
    half = rows_in.shape[0] // 2
    for first, refs in ((odd, direct), (1 - odd, other)):
        for i, ref in enumerate(refs):
            count = ref.shape[0]
            at = pl.multiple_of(first * half + i * count, count)
            rows_in[pl.ds(at, count), :] = ref[...]


def turn_rows(direct, other, after=()):
    count = len(direct)
    rows, features = 2 * count * direct[0].shape[0], direct[0].shape[1]

    def kernel(*refs):
        out, rows_in, turned = refs[2 * count :]
        gather_rows(refs[:count], refs[count : 2 * count], rows_in)
        turned[...] = rows_in[...].T
        height = features // 8
        for i, block in enumerate(weight_order()):
            at = pl.ds(pl.multiple_of(block * height, STEP), height)
            out[i * height : (i + 1) * height, :] = turned[at, :]

    return call(
        kernel,
        "turn_rows",
        [shape((features, rows), BF16)],
        [*direct, *other],
        [pltpu.VMEM((rows, features), BF16), pltpu.VMEM((features, rows), BF16)],
        after,
    )[0]


def logits_kernel(direct, other, weight, teacher, side, known, *refs):
    group = len(refs) - 8
    first, refs = refs[:group], refs[group:]
    logits, stats, rows_in, top, total, gap, picked, chosen = refs
    rows, width = logits.shape
    vocab = lax.axis_index("vocab")
    gather_rows(direct, other, rows_in)
    value = rows_in[...]

    ids = side[0:1, :] - (vocab * width).astype(F32)
    chosen[...] = spread(ids) - lax.broadcasted_iota(jnp.int32, chosen.shape, 1).astype(F32)
    for ref in (total, gap, picked):
        ref[...] = jnp.zeros(ref.shape, F32)
    inside = rows // QUARTERS
    for start, size in tiles(0, width, 5 * LANES):
        tile = jnp.dot(value, weight[:, start : start + size], preferred_element_type=F32)
        logits[:, start : start + size] = tile
        columns = range(start, start + size, LANES)
        for at in range(0, rows, BAND):
            here = slice(at, at + BAND)
            from_row = (at // inside * 2 + group) * inside + at % inside
            there = slice(from_row, from_row + BAND)
            students = [tile[here, c - start : c - start + LANES] for c in columns]
            best = functools.reduce(jnp.maximum, students)
            if start:
                last = top[here, :]
                best = jnp.maximum(best, last)
                scale = jnp.exp(last - best)
                sums = [total[there, :] * scale, gap[there, :] * scale]
                hit = picked[there, :]
            else:
                sums, hit = [0.0, 0.0], 0.0
            top[here, :] = best
            wanted = chosen[there, :]
            for c, student in zip(columns, students):
                target = teacher[there, c : c + LANES].astype(F32)
                share = jnp.exp(student - best)
                sums = [sums[0] + share, sums[1] + share * (student - target)]
                hit = hit + jnp.where(wanted == c, student, 0.0)
            total[there, :], gap[there, :], picked[there, :] = *sums, hit

    top_row = jnp.max(top[...].T, axis=0, keepdims=True)
    whole_top = spread(top_row)
    for at in range(0, rows, inside):
        here = slice(at, at + inside)
        from_row = (at // inside * 2 + group) * inside
        there = slice(from_row, from_row + inside)
        scale = jnp.exp(top[here, :] - whole_top[here, :])
        total[there, :] = total[there, :] * scale
        gap[there, :] = gap[there, :] * scale
        top[here, :] = whole_top[here, :]

    rows_known = {k: lane_sum(ref) for k, ref in ((1, total), (2, gap), (5, picked))}
    for q in range(QUARTERS):
        at = (2 * q + group) * inside
        total[at : at + inside, :] = top[q * inside : (q + 1) * inside, :]
    rows_known[0] = total[...].T[0:1, :]
    stats[...] = known[...]
    for k, row in rows_known.items():
        if first:
            lane = lax.broadcasted_iota(jnp.int32, row.shape, 1)
            row = jnp.where((lane & inside) != 0, row, first[0][k : k + 1, :])
        stats[k : k + 1, :] = row


def group_logits(direct, other, weight, teacher, side, known, first, after=()):
    rows, width = teacher.shape
    features = weight.shape[0]
    count = len(direct)

    def kernel(*refs):
        logits_kernel(refs[:count], refs[count : 2 * count], *refs[2 * count :])

    return call(
        kernel,
        "group_logits",
        [
            shape((rows // 2, width), F32),
            shape((STATS, rows), F32),
        ],
        [*direct, *other, weight, teacher, side, known, *first],
        [pltpu.VMEM((rows // 2, features), BF16)]
        + [pltpu.VMEM((rows // 2, LANES), F32)]
        + [pltpu.VMEM((rows, LANES), F32)] * 4,
        after,
        flops=LONG if first else COST,
    )


def join(parts):
    top = functools.reduce(jnp.maximum, [p[0] for p in parts])
    teacher_top = functools.reduce(jnp.maximum, [p[3] for p in parts])
    scales = [jnp.exp(p[0] - top) for p in parts]
    total = sum(s * p[1] for s, p in zip(scales, parts))
    gap = sum(s * p[2] for s, p in zip(scales, parts))
    teacher_total = sum(jnp.exp(p[3] - teacher_top) * p[4] for p in parts)
    picked = sum(p[5] for p in parts)
    return top, total, gap, teacher_top, teacher_total, picked


def over_vocab(stats, size):
    parts, done = [stats], 1
    while done < size:
        if done > 1:
            joined = join([[p[k] for k in range(6)] for p in parts])
            parts = [jnp.stack(list(joined) + [joined[0]] * (STATS - 6))]
        radix = min(4, size // done)
        parts += [xor_swap(parts[0], "vocab", k * done) for k in range(1, radix)]
        done *= radix
    return parts


def row_kernel(stats, side, counts, tokens, lses, shifts, weights):
    top, total, gap, teacher_top, teacher_total, picked = join(
        [[s[k : k + 1, :] for k in range(6)] for s in stats]
    )
    lse = top + jnp.log(total)
    diff = lse - (teacher_top + jnp.log(teacher_total))
    kl = gap / total - diff
    tokens[...] = jnp.concatenate([kl, picked - lse])
    mask_total = counts[0][0:1, 0:1] + counts[1][0:1, 0:1]
    lses[...] = spread(lse)
    shifts[...] = spread(diff + kl)
    weights[...] = spread(side[1:2, :] / jnp.maximum(mask_total, 1.0))


def slope_kernel(lses, shifts, weights, teacher, *refs, start):
    for group, (logits, slope) in enumerate(zip(refs[:2], refs[2:])):
        rows, width = slope.shape
        steps = row_steps(2 * rows, group)

        @pl.loop(0, rows // STEP, unroll=4)
        def _(i):
            here, there = steps(i)
            lse, shift, weight = lses[there, :], shifts[there, :], weights[there, :]
            for at, size in tiles(0, width, LANES):
                student = logits[here, start + at : start + at + size]
                target = teacher[there, start + at : start + at + size].astype(F32)
                value = weight * jnp.exp(student - lse) * (student - target - shift)
                slope[here, at : at + size] = value.astype(BF16)


def first_slopes(stats, side, counts, teacher, logits, hidden_t, size):
    rows = teacher.shape[0]
    features = hidden_t[0].shape[0]
    parts = len(stats)

    def kernel(*refs):
        before, (away, slope_0, slope_1, *after) = refs[: parts + 8], refs[parts + 8 :]
        side, first, second, teacher, *logits = before[parts : parts + 6]
        row_kernel(before[:parts], side, (first, second), *after)
        slope_kernel(*after[1:], teacher, *logits, slope_0, slope_1, start=0)
        weight_away_kernel(*before[parts + 6 :], slope_0, slope_1, away, start=0)

    away, *slopes, tokens, lses, shifts, weights = call(
        kernel,
        "slopes",
        [shape((features // 2, size), BF16)]
        + [shape((rows // 2, size), BF16)] * 2
        + [shape((2, rows), F32)]
        + [shape((rows, LANES), F32)] * 3,
        [*stats, side, *counts, teacher, *logits, *hidden_t],
    )
    return away, slopes, tokens, (lses, shifts, weights)


def more_slopes(columns, teacher, logits, start, size, after=()):
    rows = teacher.shape[0]
    return call(
        functools.partial(slope_kernel, start=start),
        "slopes",
        [shape((rows // 2, size), BF16)] * 2,
        [*columns, teacher, *logits],
        (),
        after,
    )


def weight_blocks(hidden_t, slopes, first, count, start, size):
    return sum(
        jnp.dot(
            left[first : first + count, :],
            right[:, start : start + size],
            preferred_element_type=F32,
        )
        for left, right in zip(hidden_t, slopes)
    )


def weight_away_kernel(*refs, start):
    hidden_t, slopes, out = refs[:2], refs[2:4], refs[4]
    out[...] = weight_blocks(hidden_t, slopes, 0, out.shape[0], start, out.shape[1]).astype(BF16)


def weight_away(hidden_t, slopes, start, size, after=()):
    features = hidden_t[0].shape[0]
    return call(
        functools.partial(weight_away_kernel, start=start),
        "weight_away",
        [shape((features // 2, size), BF16)],
        [*hidden_t, *slopes],
        (),
        after,
    )[0]


def weight_home_kernel(*refs, start):
    hidden_t, slopes, received, outs = refs[:2], refs[2:4], refs[4], refs[5:]
    count, size = outs[0].shape
    for part, out in enumerate(outs):
        value = weight_blocks(hidden_t, slopes, (2 + part) * count, count, start, size)
        value += received[part * count : (part + 1) * count, :].astype(F32)
        out[...] = value.astype(BF16)


def weight_home(hidden_t, slopes, received, start, after=()):
    count, size = received.shape
    return call(
        functools.partial(weight_home_kernel, start=start),
        "weight_home",
        [shape((count // 2, size), BF16)] * 2,
        [*hidden_t, *slopes, received],
        (),
        after,
    )


def hidden_kernel(*refs, vocab_size, groups):
    *slopes, weight, away, home, rows = refs
    blocks = vocab_size
    height = rows.shape[0] // blocks
    begin = 0
    for at_part in range(0, len(slopes), groups):
        part = slopes[at_part : at_part + groups]
        columns = slice(begin, begin + part[0].shape[1])
        begin = columns.stop
        for i, block in enumerate(hidden_order(vocab_size)):
            to = slice(i * height, (i + 1) * height)
            if groups == 1:
                at = pl.multiple_of(block * height, height)
                rows[to, columns] = part[0][pl.ds(at, height), :]
                continue
            per = vocab_size // QUARTERS // 2
            at = pl.multiple_of((block // (2 * per) * per + block % per) * height, height)
            for group, slope in enumerate(part):

                @pl.when(block // per % 2 == group)
                def _():
                    rows[to, columns] = slope[pl.ds(at, height), :]

    value = rows[...]
    middle = away.shape[0]
    for start, size in tiles(0, weight.shape[0], 2 * LANES):
        at = slice(start, start + size)
        result = lax.dot_general(
            value, weight[at, :], (((1,), (1,)), ((), ())), preferred_element_type=F32
        )
        away[:, at] = result[:middle].astype(BF16)
        home[:, at] = result[middle:]


def hidden_blocks(slopes, weight, vocab_size, after=()):
    width = weight.shape[1]
    rows = sum(s.shape[0] for s in slopes[0])
    dims = (rows // 2, weight.shape[0])
    return call(
        functools.partial(hidden_kernel, vocab_size=vocab_size, groups=len(slopes[0])),
        "hidden_grad",
        [shape(dims, BF16), shape(dims, F32)],
        [*sum(slopes, []), weight],
        [pltpu.VMEM((rows, width), BF16)],
        after,
    )


def add_kernel(kept, received, *outs):
    count = outs[0].shape[0]
    for i, out in enumerate(outs):
        at = slice(i * count, (i + 1) * count)
        out[...] = (kept[at, :].astype(F32) + received[at, :].astype(F32)).astype(BF16)


def add(kept, received, parts, after=()):
    rows, width = kept.shape
    return call(
        add_kernel,
        "add",
        [shape((rows // parts, width), BF16)] * parts,
        [kept, received],
        (),
        after,
    )


def pack_kernel(kept, received, tokens, out):
    rows, width = kept.shape
    out[:, :width] = (kept[...].astype(F32) + received[...].astype(F32)).astype(BF16)
    rest, terms = tokens[...], []
    for _ in range(3):
        terms.append(rest.astype(BF16).astype(F32))
        rest = rest - terms[-1]
    rows_of = [fold(term[k : k + 1]) for term in terms for k in range(2)]
    room = rows * (out.shape[1] - width) // LANES
    values = pad_rows(jnp.concatenate(rows_of), room).astype(BF16)
    for i in range(room // rows):
        at = width + i * LANES
        out[:, at : at + LANES] = values[i * rows : (i + 1) * rows]


def pack(kept, received, tokens, after=()):
    rows, width = kept.shape
    need = 6 * tokens.shape[1] // LANES
    outs = [shape((rows, width + -(-need // rows) * LANES), BF16)]
    return call(pack_kernel, "pack", outs, [kept, received, tokens], (), after)


def tokens_kernel(strip, *values, width):
    folded = jnp.concatenate(
        [strip[:, at : at + LANES] for at in range(width, strip.shape[1], LANES)]
    ).astype(F32)
    for k, value in enumerate(values):
        size = value.shape[1]
        value[...] = sum(unfold(folded, k + 2 * term, size) for term in range(3))


def tokens_of(strip, rows, width, after):
    outs = [shape((1, rows), F32)] * 2
    kernel = functools.partial(tokens_kernel, width=width)
    return call(kernel, "tokens_of", outs, [strip], (), after)


def finish_kernel(*refs, start, so_far):
    kept, received, out, token, source, done = refs[so_far:]
    source[...] = (kept[...].astype(F32) + received[...].astype(F32)).astype(BF16)
    token[...] = jnp.zeros(token.shape, F32)
    run_copies(copy_pairs(source, out.at[:, start : start + source.shape[1]]), done)


def finish(parts, dims, start, so_far, after):
    return call(
        functools.partial(finish_kernel, start=start, so_far=len(so_far)),
        "finish",
        [pltpu.HBM(dims, BF16), shape((8, LANES), F32)],
        list(parts),
        [pltpu.VMEM(parts[0].shape, BF16), pltpu.SemaphoreType.DMA((8,))],
        after,
        so_far,
        bool(so_far),
    )


def local(hidden, out_weight, teacher_logits, token_ids, loss_mask):
    rows, features = hidden.shape
    width = out_weight.shape[1]
    vocab_size = lax.axis_size("vocab")
    group_axes, group_size = ("role", "dp"), lax.axis_size("role") * lax.axis_size("dp")
    assert lax.axis_size("role") == 2 and lax.axis_size("dp") == 4
    assert vocab_size & (vocab_size - 1) == 0 and vocab_size >= QUARTERS

    ids, mask = token_ids.reshape(1, rows), loss_mask.reshape(1, rows)
    pieces = []
    for k, some in enumerate([[(0, 0)], [(0, 1)], [(1, 0), (1, 1)]]):
        pieces += pick_rows(hidden, some, (ids, mask) if k == 1 else (), after=pieces[-1:])
    direct = [xor_swap(piece, "role", 1) for piece in pieces]
    known = teacher_stats(teacher_logits, after=pieces[1:2])
    direct[0] = pass_on(direct[0], [known])
    direct[1], side = unpack_rows(direct[1], rows)
    count = count_rows(side, mask)
    count = sum_rows(count, xor_swap(count, "dp", 1))
    direct[3] = pass_on(direct[3], [count])
    counts = [count, xor_swap(count, "dp", 2)]
    other = [xor_swap(piece, "vocab", 1) for piece in direct]

    logits, hidden_t, stats = [], [], []
    for group in range(2):
        pair = slice(2 * group, 2 * group + 2)
        done = group_logits(
            direct[pair],
            other[pair],
            out_weight,
            teacher_logits,
            side,
            known,
            stats[-1:],
            after=counts[1:] if group else direct[3:],
        )
        for values, value in zip((logits, stats), done):
            values.append(value)
        hidden_t.append(turn_rows(direct[pair], other[pair], after=stats[group:]))
    chunks = column_chunks(width, (7, 6, 6))
    split = chunks[1][0]
    last, slopes, tokens, columns = first_slopes(
        over_vocab(stats[1], vocab_size), side, counts, teacher_logits, logits, hidden_t, split
    )
    ranges = [(0, list(slopes))]

    def slope_step(last):
        slopes = more_slopes(columns, teacher_logits, logits, split, width - split, after=[last])
        ranges.append((split, list(slopes)))
        return slopes[1]

    by_group = vocab_size == QUARTERS
    home, hidden_in = [], []

    def hidden_step(last):
        k = len(home)
        if k == 0 or by_group:
            some = [s[k : k + 1] if by_group else s for _, s in ranges]
            last, kept = hidden_blocks(some, out_weight, vocab_size, after=[last])
            home.append(kept)
            hidden_in.append(xor_swap(last, "vocab", 1))
        return last

    arrived, near = [], []

    def chunk_of(k):
        start, size = chunks[k]
        begin, slopes = ranges[min(k, 1)]
        return slopes, start - begin, size

    def away_step(last):
        if arrived:
            last = weight_away(hidden_t, *chunk_of(len(arrived)), after=[last])
        arrived.append(exchange(last, group_axes, group_size, lambda i: i ^ 1))
        return last

    def near_step(last):
        k = len(near)
        slopes, start, _ = chunk_of(k)
        leaving, last = weight_home(hidden_t, slopes, arrived[k], start, after=[last])
        near.append((last, exchange(leaving, group_axes, group_size, near_of)))
        return last

    far, grad_weight, returned, outs = [], [], [], []

    def far_step(last):
        kept, received = near[len(far)]
        leaving, last = add(kept, received, 2, after=[last])
        far.append((last, exchange(leaving, group_axes, group_size, far_of)))
        return last

    def weight_step(last):
        k = len(grad_weight)
        dims = (features // group_size, width)
        result, last = finish(far[k], dims, chunks[k][0], grad_weight[-1:], [last])
        grad_weight.append(result)
        return last

    halved = []

    def halve_step(last):
        if len(halved) < len(home):
            k = len(halved)
            leaving, last = add(home[k], hidden_in[k], 2, after=[last])
            halved.append((last, xor_swap(leaving, "vocab", 2)))
        return last

    def return_step(last):
        if len(returned) < len(home):
            kept, received = halved[len(returned)]
            bit = 4
            while bit < vocab_size:
                leaving, last = add(kept, received, 2, after=[last])
                kept, received = last, xor_swap(leaving, "vocab", bit)
                bit *= 2
            if returned:
                (last,) = add(kept, received, 1, after=[last])
            else:
                (last,) = pack(kept, received, tokens, after=[last])
            returned.append(xor_swap(last, "role", 1))
        return last

    def tokens_step(last):
        outs.extend(tokens_of(returned[0], rows, features, [last]))
        return outs[0]

    steps = {
        "s": slope_step,
        "a": away_step,
        "n": near_step,
        "h": hidden_step,
        "f": far_step,
        "v": halve_step,
        "r": return_step,
        "w": weight_step,
        "t": tokens_step,
    }
    for name in "asaanhnnhfvrfvfwwrtw":
        last = steps[name](last)

    grad_hidden = jnp.concatenate([r[:, :features] for r in returned])
    return outs[0].reshape(rows), outs[1].reshape(rows), grad_hidden, grad_weight[-1]


def solution(mesh):
    return jax.shard_map(
        local,
        mesh=mesh,
        in_specs=(
            P(("role", "dp"), None),
            P(None, "vocab"),
            P(("role", "dp"), "vocab"),
            P(("role", "dp")),
            P(("role", "dp")),
        ),
        out_specs=(
            P(("role", "dp")),
            P(("role", "dp")),
            P(("role", "dp", "vocab"), None),
            P(("role", "dp"), "vocab"),
        ),
        check_vma=False,
    )
```
